256 devices in a mesh: space: 64 (over z, x, core), blk: 4 (over y).
Axes of the slice: x: 4, y: 4, z: 8, core: 2. Of those that a mesh axis runs over, the one named last changes fastest.
Arguments:
- start: float32 [262144, 128], P('space', 'blk')
- faces: int32 [4096, 6], P('space'), may hold values from -1 to 4095, as said below
- cavity: int32 [4096], P('space'), may hold values 0 or 1
- blocks: float32 [4096, 7, 64, 64], P('space'), as said below
Outputs:
- next_basis: float32 [262144, 128], P('space', 'blk')
- coefficients: float32 [5, 128, 128], P(None, None, 'blk')
The draws below stay inside these ranges and needn't reach their ends.
Inputs may be any that keep to these rules, and one draw needn't show every extreme that they name: Elements are numbered layer by layer along the slab's third dimension, 64 to a layer, in an order within each layer that the draw sets; faces 0 to 5 look towards falling and rising first, second and third coordinates; an entry is -1 exactly where the face lies on the slab's outer boundary, else the element across the face, which lies in the same layer or the layers just below and above. Where faces[e, f] = n >= 0, blocks[e, f + 1] is the transpose of n's block for the opposite face; blocks[e, 0] is symmetric.
All inputs are finite; a program needn't handle non-finite values. No bound on the sum of `cavity` on one device may be relied on, other than what follows from the above.
Results may differ from the reference program's by a relative error of at most 0.0002.
Values sent between devices are 32-bit elements; how exact they have to be, the bound alone decides.
A program may use at most 128 MiB of HBM per device.

```python
import math
import jax
import jax.numpy as jnp
from jax import lax

P_SIZE = 64
K = 128
GX = 8
GY = 8
ELEMS = 4096
NDOF = 262144


def pattern(key):
    per_layer = GX * GY
    layer_total = ELEMS // per_layer
    subkeys = jax.random.split(jax.random.fold_in(key, 5), layer_total)
    orders = jax.vmap(lambda subkey: jax.random.permutation(subkey, per_layer))(subkeys).astype(jnp.int32)
    pos_z = jnp.arange(layer_total, dtype=jnp.int32)[:, None]
    places = jnp.arange(per_layer, dtype=jnp.int32)[None, :]
    pos_x = places // GY
    pos_y = places % GY

    def element_at(zz, xx, yy, inside):
        zc = jnp.clip(zz, 0, layer_total - 1)
        pc = jnp.clip(xx, 0, GX - 1) * GY + jnp.clip(yy, 0, GY - 1)
        zc, pc = jnp.broadcast_arrays(zc, pc)
        found = zc * per_layer + orders[zc, pc]
        return jnp.where(inside, found, -1)
    by_position = jnp.stack([element_at(pos_z, pos_x - 1, pos_y, pos_x > 0), element_at(pos_z, pos_x + 1, pos_y, pos_x < GX - 1), element_at(pos_z, pos_x, pos_y - 1, pos_y > 0), element_at(pos_z, pos_x, pos_y + 1, pos_y < GY - 1), element_at(pos_z - 1, pos_x, pos_y, pos_z > 0), element_at(pos_z + 1, pos_x, pos_y, pos_z < layer_total - 1)], axis=-1)
    position_of = jnp.argsort(orders, axis=1).astype(jnp.int32)
    faces = jnp.take_along_axis(by_position, position_of[:, :, None], axis=1)
    return faces.reshape(ELEMS, 6).astype(jnp.int32)


def draw_faces(key, part):
    return pattern(key)


def draw_blocks(key, part):
    faces = pattern(key)
    key = jax.random.fold_in(key, 7)
    key_one, key_two, key_three = jax.random.split(key, 3)
    spread = 1.0 / math.sqrt(P_SIZE)
    noise = jax.random.normal(key_one, (ELEMS, P_SIZE, P_SIZE), jnp.float32) * (0.5 * spread)
    diagonal = 2.0 * jnp.eye(P_SIZE, dtype=jnp.float32)[None] + noise + jnp.transpose(noise, (0, 2, 1))
    couplings = jax.random.normal(key_two, (ELEMS, 3, P_SIZE, P_SIZE), jnp.float32) * (0.6 * spread)
    padding = jax.random.normal(key_three, (ELEMS, 3, P_SIZE, P_SIZE), jnp.float32) * (0.6 * spread)
    parts_list = [diagonal]
    for direction in range(3):
        lower_id = faces[:, 2 * direction]
        mirrored = jnp.transpose(couplings[jnp.clip(lower_id, 0, ELEMS - 1), direction], (0, 2, 1))
        parts_list.append(jnp.where((lower_id >= 0)[:, None, None], mirrored, padding[:, direction]))
        parts_list.append(couplings[:, direction])
    return jnp.stack(parts_list, axis=1).astype(jnp.float32)


def draw_start(key, part):
    key = jax.random.fold_in(key, 11)
    key_one, key_two, key_three = jax.random.split(key, 3)
    col_scale = jnp.exp(jax.random.uniform(key_three, (1, K), jnp.float32) * math.log(10.0))
    entries = jax.random.normal(key_one, (NDOF, K), jnp.float32)
    row_scale = jnp.exp(jax.random.uniform(key_two, (NDOF, 1), jnp.float32) * math.log(10.0))
    return (0.1 * entries * row_scale * col_scale).astype(jnp.float32)


def touch_ends(array, rng, least, largest):
    longest = array.shape.index(max(array.shape))
    spots = []
    for shift in (0, 1):
        where = [jax.random.randint(jax.random.fold_in(rng, axis), (), 0, length) for axis, length in enumerate(array.shape)]
        where[longest] = (where[longest] + shift) % array.shape[longest]
        spots.append(tuple(where))
    return array.at[spots[0]].set(least).at[spots[1]].set(largest)


def setup_inputs(seed: int = 0) -> dict:
    key_of = jax.random.split(jax.random.key(seed), 5)
    return {
        "start": draw_start(jax.random.fold_in(key_of[4], 71), 0),
        "faces": draw_faces(jax.random.fold_in(key_of[4], 71), 0),
        "cavity": touch_ends((jax.random.randint(key_of[2], (ELEMS,), 0, 16) < 1).astype(jnp.int32), jax.random.fold_in(key_of[2], 1), 0, 1),
        "blocks": draw_blocks(jax.random.fold_in(key_of[4], 71), 0),
    }


def apply_stiffness(vectors, faces, solid_mask, blocks):
    masked = vectors.reshape(ELEMS, P_SIZE, K) * solid_mask[:, None, None]
    result_sum = jnp.einsum('epq,eqc->epc', blocks[:, 0], masked, precision=lax.Precision.HIGHEST)
    has_face = faces >= 0
    face_index = jnp.where(has_face, faces, 0).astype(jnp.int32)
    face_weight = has_face.astype(jnp.float32)
    for face_num in range(6):
        neighbours = masked[face_index[:, face_num]] * face_weight[:, face_num][:, None, None]
        result_sum = result_sum + jnp.einsum('epq,eqc->epc', blocks[:, face_num + 1], neighbours, precision=lax.Precision.HIGHEST)
    return (result_sum * solid_mask[:, None, None]).reshape(NDOF, K)

def factor(block_now):
    gram_matrix = lax.dot_general(block_now.astype(jnp.float32), block_now.astype(jnp.float32), (((0,), (0,)), ((), ())), precision=lax.Precision.HIGHEST, preferred_element_type=jnp.float32)
    lower_factor = jnp.linalg.cholesky(gram_matrix)
    lower_inverse = jax.scipy.linalg.solve_triangular(lower_factor, jnp.eye(K, dtype=jnp.float32), lower=True)
    return (jnp.dot(block_now.astype(jnp.float32), lower_inverse.T.astype(jnp.float32), precision=lax.Precision.HIGHEST, preferred_element_type=jnp.float32), lower_factor.T)

def inner_sum(left, right):
    return lax.dot_general(left.astype(jnp.float32), right.astype(jnp.float32), (((0,), (0,)), ((), ())), precision=lax.Precision.HIGHEST, preferred_element_type=jnp.float32)

def times(left, right):
    return jnp.dot(left.astype(jnp.float32), right.astype(jnp.float32), precision=lax.Precision.HIGHEST, preferred_element_type=jnp.float32)

def reference(start, faces, cavity, blocks):
    solid_mask = (1 - cavity).astype(jnp.float32)
    basis_one, start_factor = factor(start)
    residue = apply_stiffness(basis_one, faces, solid_mask, blocks)
    alpha_one = inner_sum(basis_one, residue)
    residue = residue - times(basis_one, alpha_one)
    basis_two, beta_one = factor(residue)
    residue = apply_stiffness(basis_two, faces, solid_mask, blocks) - times(basis_one, beta_one.T)
    alpha_two = inner_sum(basis_two, residue)
    residue = residue - times(basis_two, alpha_two)
    basis_three, beta_two = factor(residue)
    return (basis_three, jnp.stack([start_factor, alpha_one, beta_one, alpha_two, beta_two]))
```

```python
import jax
import jax.numpy as jnp
from jax import lax
from jax.experimental import pallas as pl
from jax.experimental.pallas import tpu as pltpu
from jax.sharding import PartitionSpec as P

GX = 8
GY = 8
CORES = 2
XS = 4
ZS = 8
YS = 4
MESH = pl.DeviceIdType.MESH


def reduce_kernel(part, out, near, far, done, send_sem, recv_sem):
    half = part.shape[0] // CORES
    space = lax.axis_index("space")
    blk = lax.axis_index("blk")
    core = lax.rem(space, CORES)
    spot = lax.rem(space, XS * CORES)
    plane = space // (XS * CORES)
    base = plane * (XS * CORES)
    quad = blk * CORES + core

    barrier = pltpu.get_barrier_semaphore()
    near_ids = []
    far_ids = []
    done_ids = []
    for step in range(1, 8):
        near_ids.append(lax.rem(spot + step, 8))
        far_ids.append(lax.rem(plane + step, 8))
        done_ids.append(lax.rem(quad + step, 8))
    for step in range(7):
        pl.semaphore_signal(barrier, inc=1, device_id=(base + near_ids[step], blk), device_id_type=MESH)
        pl.semaphore_signal(barrier, inc=1, device_id=(far_ids[step] * 8 + spot, blk), device_id_type=MESH)
        pl.semaphore_signal(
            barrier,
            inc=1,
            device_id=(space - core + lax.rem(done_ids[step], CORES), done_ids[step] // CORES),
            device_id_type=MESH,
        )
    pl.semaphore_wait(barrier, 21)

    def exchange(stage, sources, slots, mine, devices):
        copies = []
        for step in range(7):
            copy = pltpu.make_async_remote_copy(
                src_ref=sources[step],
                dst_ref=slots.at[mine],
                send_sem=send_sem.at[stage, step],
                recv_sem=recv_sem.at[stage, step],
                device_id=devices[step],
                device_id_type=MESH,
            )
            copy.start()
            copies.append(copy)
        return copies

    def total(slots):
        value = slots[0]
        for slot in range(1, 8):
            value = value + slots[slot]
        return value

    sources = []
    devices = []
    for step in range(7):
        side = lax.rem(near_ids[step], CORES)
        sources.append(part.at[pl.ds(pl.multiple_of(side * half, 8), half)])
        devices.append((base + near_ids[step], blk))
    copies = exchange(0, sources, near, spot, devices)
    near[spot] = part[pl.ds(pl.multiple_of(core * half, 8), half)]
    for copy in copies:
        copy.wait()
    far[plane] = total(near)
    copies = exchange(
        1, [far.at[plane]] * 7, far, plane, [(far_ids[step] * 8 + spot, blk) for step in range(7)]
    )
    for copy in copies:
        copy.wait()
    done[quad] = total(far)
    copies = exchange(
        2,
        [done.at[quad]] * 7,
        done,
        quad,
        [
            (space - core + lax.rem(done_ids[step], CORES), done_ids[step] // CORES)
            for step in range(7)
        ],
    )
    for copy in copies:
        copy.wait()
    for slot in range(8):
        out[slot] = done[slot]


def reduce_all(part, collective_id):
    rows, cols = part.shape
    half = rows // CORES
    out = pl.pallas_call(
        reduce_kernel,
        out_shape=jax.ShapeDtypeStruct((8, half, cols), jnp.float32),
        in_specs=[pl.BlockSpec(memory_space=pltpu.VMEM)],
        out_specs=pl.BlockSpec(memory_space=pltpu.VMEM),
        scratch_shapes=[
            pltpu.VMEM((8, half, cols), jnp.float32),
            pltpu.VMEM((8, half, cols), jnp.float32),
            pltpu.VMEM((8, half, cols), jnp.float32),
            pltpu.SemaphoreType.DMA((3, 7)),
            pltpu.SemaphoreType.DMA((3, 7)),
        ],
        compiler_params=pltpu.CompilerParams(collective_id=collective_id, has_side_effects=True),
    )(part)
    return out.reshape(YS, rows, cols)


def padded_2(block, width):
    count = lax.axis_size("space")
    forward = [(i, i + 1) for i in range(count - 1)]
    backward = [(target, source) for source, target in forward]
    low = lax.ppermute(lax.slice_in_dim(block, block.shape[0] - width, None, axis=0), "space", forward)
    high = lax.ppermute(lax.slice_in_dim(block, 0, width, axis=0), "space", backward)
    return jnp.concatenate([low, block, high], axis=0)


def cross(left, right):
    return lax.dot_general(
        left,
        right,
        (((1,), (1,)), ((), ())),
        precision=lax.Precision.HIGHEST,
        preferred_element_type=jnp.float32,
    )


def times(left, right):
    return jnp.dot(left, right, precision=lax.Precision.HIGHEST, preferred_element_type=jnp.float32)


def lower_and_inverse(gram):
    lower = jnp.linalg.cholesky(gram)
    inverse = jax.scipy.linalg.solve_triangular(
        lower, jnp.eye(lower.shape[0], dtype=jnp.float32), lower=True
    )
    return lower, inverse


def local(start, faces, cavity, blocks):
    elem_count = blocks.shape[0]
    dof_width = blocks.shape[-1]
    narrow = start.shape[1]
    layer_size = GX * GY
    solid_mask = (1 - cavity).astype(jnp.float32)
    has_face = faces >= 0
    local_index = jnp.where(has_face, faces - lax.axis_index("space") * elem_count + layer_size, 0)
    face_weight = has_face.astype(jnp.float32)
    own_start = lax.axis_index("blk") * narrow
    own_index = layer_size + jnp.arange(elem_count, dtype=jnp.int32)
    all_index = jnp.concatenate([own_index[:, None], local_index], axis=1)
    all_weight = jnp.concatenate([jnp.ones((elem_count, 1), jnp.float32), face_weight], axis=1)

    def operate(vectors):
        masked = vectors.T.reshape(elem_count, dof_width, narrow) * solid_mask[:, None, None]
        padded = padded_2(masked, layer_size)
        around = jnp.take(padded, all_index, axis=0) * all_weight[:, :, None, None]
        product = jnp.einsum("efpq,efqc->epc", blocks, around, precision=lax.Precision.HIGHEST)
        return (product * solid_mask[:, None, None]).reshape(-1, narrow).T

    def own(matrix):
        return lax.dynamic_slice_in_dim(matrix, own_start, narrow, 0)

    def gather(rows):
        return lax.all_gather(rows, "blk", axis=0, tiled=True)

    def square(sums, which):
        return sums[:, which * narrow : (which + 1) * narrow].reshape(YS * narrow, -1)

    start_own = start.T
    start_all = gather(start_own)
    image_own = operate(start_own)
    image_all = gather(image_own)
    sums = reduce_all(cross(jnp.concatenate([start_own, image_own]), start_all), 1)
    lower_0, inverse_0 = lower_and_inverse(square(sums, 0))
    alpha_one = times(times(inverse_0, square(sums, 1)), inverse_0.T)
    basis_one = times(inverse_0, start_all)
    residue = times(inverse_0, image_all) - times(alpha_one, basis_one)

    residue_own = own(residue)
    image_own = operate(residue_own)
    image_all = gather(image_own)
    part = jnp.concatenate(
        [cross(jnp.concatenate([residue_own, image_own]), residue), cross(residue_own, basis_one)]
    )
    sums = reduce_all(part, 2)
    lower_1, inverse_1 = lower_and_inverse(square(sums, 0))
    skew = times(inverse_1, square(sums, 2))
    basis_two = times(inverse_1, residue)
    alpha_two = times(times(inverse_1, square(sums, 1)), inverse_1.T) - times(lower_1.T, skew.T)
    residue = (
        times(inverse_1, image_all) - times(lower_1.T, basis_one) - times(alpha_two, basis_two)
    )

    sums = reduce_all(cross(own(residue), residue), 3)
    lower_2, inverse_2 = lower_and_inverse(square(sums, 0))
    basis_three = times(own(inverse_2), residue)
    coefficients = jnp.stack(
        [
            own(lower_0).T,
            own(alpha_one).T,
            own(lower_1).T,
            own(alpha_two).T,
            own(lower_2).T,
        ]
    )
    return basis_three.T, coefficients


def solution(mesh):
    in_specs = (P("space", "blk"), P("space", None), P("space"), P("space", None, None, None))
    out_specs = (P("space", "blk"), P(None, None, "blk"))
    return jax.shard_map(local, mesh=mesh, in_specs=in_specs, out_specs=out_specs, check_vma=False)
```

```python
import jax
import jax.numpy as jnp
from jax import lax
from jax.experimental import pallas as pl
from jax.experimental.pallas import tpu as pltpu
from jax.sharding import PartitionSpec as P

LAYER = 64
DOF = 64
ROWS = LAYER * DOF
K = 128
CORES = 2
XS = 4
ZS = 8
YS = 4
SPACE = ZS * XS * CORES
NARROW = K // YS
SIDES = 7
NONE = 3 * LAYER
WIDE = 32
SUB = 8
CHUNK = 512
STAGED = 16
MESH = pl.DeviceIdType.MESH
F32 = jnp.float32
BF16 = jnp.bfloat16


def dot(left, right, left_dim, right_dim):
    return lax.dot_general(
        left,
        right,
        (((left_dim,), (right_dim,)), ((), ())),
        precision=lax.Precision.HIGHEST,
        preferred_element_type=F32,
    )


def times(left, right):
    return dot(left, right, 1, 0)


def cross(left, right):
    return dot(left, right, 1, 1)


def split(value):
    first = value.astype(BF16)
    rest = value - first.astype(F32)
    second = rest.astype(BF16)
    return first, second, (rest - second.astype(F32)).astype(BF16)


def eliminate(gram, unit, first):
    shape = gram.shape
    row_id = lax.broadcasted_iota(jnp.int32, shape, 0)
    for sub in range(0, WIDE, SUB):
        columns = [
            jnp.broadcast_to(gram[:, first + sub + j : first + sub + j + 1], shape)
            for j in range(SUB)
        ]
        for j in range(SUB):
            k = sub + j
            scale = lax.rsqrt(jnp.broadcast_to(columns[j][k : k + 1], shape))
            pivot_gram = jnp.broadcast_to(gram[k : k + 1], shape) * scale
            pivot_unit = jnp.broadcast_to(unit[k : k + 1], shape) * scale
            factor = columns[j] * scale
            below = jnp.where(row_id > k, factor, 0.0)
            for other in range(j + 1, SUB):
                near = jnp.broadcast_to(factor[sub + other : sub + other + 1], shape)
                columns[other] = columns[other] - below * near
            gram = jnp.where(row_id == k, pivot_gram, gram - below * pivot_gram)
            unit = jnp.where(row_id == k, pivot_unit, unit - below * pivot_unit)
    return gram, unit


def factor_gram(gram_ref, upper, inverse):
    row_id = lax.broadcasted_iota(jnp.int32, (WIDE, K), 0)
    col_id = lax.broadcasted_iota(jnp.int32, (WIDE, K), 1)
    for first in range(0, K, WIDE):
        rows = pl.ds(first, WIDE)
        gram = gram_ref[rows, :]
        unit = jnp.where(row_id + first == col_id, 1.0, 0.0)
        if first:
            above_gram = upper[pl.ds(0, first), :]
            above_unit = inverse[pl.ds(0, first), :]
            left = above_gram[:, first : first + WIDE]
            gram = gram - dot(left, above_gram, 0, 0)
            unit = unit - dot(left, above_unit, 0, 0)
        gram, unit = eliminate(gram, unit, first)
        upper[rows, :] = jnp.where(row_id + first <= col_id, gram, 0.0)
        inverse[rows, :] = unit


def prepare(staged, packed, base):
    def body(elem, carry):
        for pair in range(4):
            if pair < 3:
                right = staged[elem, 2 * pair + 1]
            else:
                right = jnp.zeros((DOF, DOF), F32)
            both = jnp.concatenate([staged[elem, 2 * pair], right], axis=1)
            for piece, value in enumerate(split(both)):
                packed[base + elem, piece, :, pair * 128 : (pair + 1) * 128] = value
        return carry

    lax.fori_loop(0, STAGED, body, 0, unroll=2)


def spread(source, elems, base):
    is_low = lax.broadcasted_iota(jnp.int32, (NARROW, 2 * DOF), 1) < DOF

    def body(pair, carry):
        straight = source[:, pl.ds(pl.multiple_of(pair * 128, 128), 128)]
        turned = pltpu.roll(straight, DOF, 1)
        for side, low, high in ((0, straight, turned), (1, turned, straight)):
            place = base + 2 * pair + side
            for piece, value in enumerate(split(jnp.where(is_low, low, 0.0))):
                elems[0, place, piece] = value
            for piece, value in enumerate(split(jnp.where(is_low, 0.0, high))):
                elems[1, place, piece] = value
        return carry

    lax.fori_loop(0, LAYER // 2, body, 0, unroll=2)


def operate(index, elems, packed, mask, out, own_rows):
    def product(left, right):
        return lax.dot_general(
            left, right, (((1,), (1,)), ((), ())), preferred_element_type=F32
        )

    def one(elem):
        at = [index[elem * SIDES + side] for side in range(SIDES)]
        pieces = []
        for piece in range(3):
            pairs = [
                elems[0, at[2 * pair], piece] + elems[1, at[2 * pair + 1], piece]
                for pair in range(3)
            ]
            pairs.append(elems[0, at[6], piece])
            pieces.append(jnp.concatenate(pairs, axis=1))
        three = product(jnp.concatenate(pieces, axis=0), packed[elem, 0])
        two = product(jnp.concatenate(pieces[:2], axis=0), packed[elem, 1])
        last = product(pieces[0], packed[elem, 2])
        small = three[2 * NARROW :] + two[NARROW:] + last
        return three[:NARROW] + (three[NARROW : 2 * NARROW] + two[:NARROW] + small)

    def body(pair, carry):
        both = jnp.concatenate([one(2 * pair), one(2 * pair + 1)], axis=1)
        cols = pl.ds(pl.multiple_of(pair * 128, 128), 128)
        out[own_rows, cols] = both * mask[:, cols]
        return carry

    lax.fori_loop(0, LAYER // 2, body, 0, unroll=4)


def kernel(
    index,
    start,
    mask,
    blocks,
    basis_out,
    coef_out,
    basis,
    image,
    second,
    send_0,
    low_0,
    high_0,
    send_1,
    low_1,
    high_1,
    elems,
    packed,
    staged,
    near_0,
    far_0,
    done_0,
    near_1,
    far_1,
    done_1,
    near_2,
    far_2,
    done_2,
    part_0,
    part_1,
    part_2,
    gram,
    upper,
    inverse,
    alpha,
    flip,
    stage_sem,
    halo_send,
    halo_recv,
    rows_send,
    rows_recv,
    sums_send,
    sums_recv,
):
    space = lax.axis_index("space")
    blk = lax.axis_index("blk")
    core = lax.rem(space, CORES)
    spot = lax.rem(space, XS * CORES)
    plane = space // (XS * CORES)
    plane_base = plane * (XS * CORES)
    quad = blk * CORES + core
    own_rows = pl.ds(pl.multiple_of(blk * NARROW, NARROW), NARROW)
    above = (lax.rem(space + 1, SPACE), blk)
    below = (lax.rem(space + SPACE - 1, SPACE), blk)
    near_ids = [lax.rem(spot + step, 8) for step in range(1, 8)]
    near_devices = [(plane_base + near, blk) for near in near_ids]
    far_devices = [(lax.rem(plane + step, 8) * 8 + spot, blk) for step in range(1, 8)]
    quads = [lax.rem(quad + step, 8) for step in range(1, 8)]
    done_devices = [(space - core + lax.rem(q, CORES), q // CORES) for q in quads]

    def stage_copy(part):
        return pltpu.make_async_copy(
            blocks.at[pl.ds(part * STAGED, STAGED)], staged.at[part % 2], stage_sem.at[part % 2]
        )

    stage_copy(0).start()
    stage_copy(1).start()
    barrier = pltpu.get_barrier_semaphore()
    for device in near_devices + far_devices + done_devices + [above, below]:
        pl.semaphore_signal(barrier, inc=1, device_id=device, device_id_type=MESH)
    basis[own_rows, :] = start[...]
    send_0[...] = start[...] * mask[...]
    pl.semaphore_wait(barrier, 23)

    def halo(call, source, low, high):
        copies = [
            pltpu.make_async_remote_copy(
                src_ref=source,
                dst_ref=target,
                send_sem=halo_send.at[call, way],
                recv_sem=halo_recv.at[call, way],
                device_id=device,
                device_id_type=MESH,
            )
            for way, target, device in ((0, low, above), (1, high, below))
        ]
        for copy in copies:
            copy.start()
        return copies

    def gather(call, array):
        copies = []
        for step in range(1, YS):
            copy = pltpu.make_async_remote_copy(
                src_ref=array.at[own_rows],
                dst_ref=array.at[own_rows],
                send_sem=rows_send.at[call, step - 1],
                recv_sem=rows_recv.at[call, step - 1],
                device_id=(space, lax.rem(blk + step, YS)),
                device_id_type=MESH,
            )
            copy.start()
            copies.append(copy)
        return copies

    def wait(copies):
        for copy in copies:
            copy.wait()

    def exchange(call, stage, sources, slots, mine, devices):
        copies = []
        for step in range(7):
            copy = pltpu.make_async_remote_copy(
                src_ref=sources[step],
                dst_ref=slots.at[mine],
                send_sem=sums_send.at[call, stage, step],
                recv_sem=sums_recv.at[call, stage, step],
                device_id=devices[step],
                device_id_type=MESH,
            )
            copy.start()
            copies.append(copy)
        return copies

    def total(slots):
        value = slots[0]
        for slot in range(1, 8):
            value = value + slots[slot]
        return value

    def reduce_all(call, part, near, far, done):
        half = part.shape[0] // CORES
        sources = [
            part.at[pl.ds(pl.multiple_of(lax.rem(spot_id, CORES) * half, 8), half)]
            for spot_id in near_ids
        ]
        copies = exchange(call, 0, sources, near, spot, near_devices)
        near[spot] = part[pl.ds(pl.multiple_of(core * half, 8), half), :]
        wait(copies)
        far[plane] = total(near)
        wait(exchange(call, 1, [far.at[plane]] * 7, far, plane, far_devices))
        done[quad] = total(far)
        wait(exchange(call, 2, [done.at[quad]] * 7, done, quad, done_devices))

    def square(done, which):
        rows = []
        for member in range(YS):
            panel = jnp.concatenate([done[2 * member], done[2 * member + 1]], axis=0)
            rows.append(panel[which * NARROW : (which + 1) * NARROW])
        return jnp.concatenate(rows, axis=0)

    def over_chunks(body, init):
        def step(chunk, carry):
            return body(pl.ds(pl.multiple_of(chunk * CHUNK, CHUNK), CHUNK), carry)

        return lax.fori_loop(0, ROWS // CHUNK, step, init)

    def keep_upper(which):
        flip[...] = upper[...].T
        coef_out[which] = flip[own_rows, :]

    halo_copies = halo(0, send_0, low_0, high_0)
    start_copies = gather(0, basis)
    for part in range(LAYER // STAGED):
        stage_copy(part).wait()
        prepare(staged.at[part % 2], packed, part * STAGED)
        if part + 2 < LAYER // STAGED:
            stage_copy(part + 2).start()
    for which in range(2):
        for piece in range(3):
            elems[which, NONE, piece] = jnp.zeros((NARROW, 2 * DOF), BF16)
    spread(send_0, elems, LAYER)
    wait(halo_copies)
    spread(low_0, elems, 0)
    spread(high_0, elems, 2 * LAYER)
    operate(index, elems, packed, mask, image, own_rows)
    image_copies = gather(1, image)
    wait(start_copies)

    def start_products(cols, carry):
        left = jnp.concatenate([basis[own_rows, cols], image[own_rows, cols]], axis=0)
        return carry + cross(left, basis[:, cols])

    part_0[...] = over_chunks(start_products, jnp.zeros(part_0.shape, F32))
    reduce_all(0, part_0, near_0, far_0, done_0)
    gram[...] = square(done_0, 0)
    factor_gram(gram, upper, inverse)
    alpha[...] = cross(times(inverse[...], square(done_0, 1)), inverse[...])
    coef_out[1] = alpha[own_rows, :]
    keep_upper(0)
    wait(image_copies)

    def first_residue(cols, carry):
        vectors = times(inverse[...], basis[:, cols])
        basis[:, cols] = vectors
        image[:, cols] = times(inverse[...], image[:, cols]) - times(alpha[...], vectors)
        return carry

    over_chunks(first_residue, 0)

    send_1[...] = image[own_rows, :] * mask[...]
    halo_copies = halo(1, send_1, low_1, high_1)
    spread(send_1, elems, LAYER)
    wait(halo_copies)
    spread(low_1, elems, 0)
    spread(high_1, elems, 2 * LAYER)
    operate(index, elems, packed, mask, second, own_rows)
    second_copies = gather(2, second)

    def residue_products(cols, carry):
        left = jnp.concatenate([image[own_rows, cols], second[own_rows, cols]], axis=0)
        return (
            carry[0] + cross(left, image[:, cols]),
            carry[1] + cross(image[own_rows, cols], basis[:, cols]),
        )

    products = over_chunks(
        residue_products, (jnp.zeros((2 * NARROW, K), F32), jnp.zeros((NARROW, K), F32))
    )
    part_1[pl.ds(0, 2 * NARROW), :] = products[0]
    part_1[pl.ds(2 * NARROW, NARROW), :] = products[1]
    reduce_all(1, part_1, near_1, far_1, done_1)
    gram[...] = square(done_1, 0)
    factor_gram(gram, upper, inverse)
    skew = times(inverse[...], square(done_1, 2))
    inner = cross(times(inverse[...], square(done_1, 1)), inverse[...])
    alpha[...] = inner - cross(upper[...], skew)
    coef_out[3] = alpha[own_rows, :]
    keep_upper(2)
    wait(second_copies)

    def second_residue(cols, carry):
        vectors = times(inverse[...], image[:, cols])
        value = times(inverse[...], second[:, cols]) - times(upper[...], basis[:, cols])
        second[:, cols] = value - times(alpha[...], vectors)
        return carry

    over_chunks(second_residue, 0)

    def last_products(cols, carry):
        return carry + cross(second[own_rows, cols], second[:, cols])

    part_2[...] = over_chunks(last_products, jnp.zeros(part_2.shape, F32))
    reduce_all(2, part_2, near_2, far_2, done_2)
    gram[...] = square(done_2, 0)
    factor_gram(gram, upper, inverse)
    keep_upper(4)

    def last_basis(cols, carry):
        basis_out[:, cols] = times(inverse[own_rows, :], second[:, cols])
        return carry

    over_chunks(last_basis, 0)


def local(start, faces, cavity, blocks):
    elem_count = blocks.shape[0]
    shift = LAYER - lax.axis_index("space") * elem_count
    beside = jnp.where(faces >= 0, faces + shift, NONE)
    here = LAYER + jnp.arange(elem_count, dtype=jnp.int32)
    index = jnp.concatenate([here[:, None], beside], axis=1).reshape(-1)
    mask = jnp.repeat((1 - cavity).astype(F32), DOF)[None, :]
    vmem = pl.BlockSpec(memory_space=pltpu.VMEM)

    def slots(rows):
        return [pltpu.VMEM((8, rows // CORES, K), F32)] * 3

    basis, coefficients = pl.pallas_call(
        kernel,
        out_shape=(
            jax.ShapeDtypeStruct((NARROW, ROWS), F32),
            jax.ShapeDtypeStruct((5, NARROW, K), F32),
        ),
        in_specs=[
            pl.BlockSpec(memory_space=pltpu.SMEM),
            vmem,
            vmem,
            pl.BlockSpec(memory_space=pl.ANY),
        ],
        out_specs=(vmem, vmem),
        scratch_shapes=[pltpu.VMEM((K, ROWS), F32)] * 3
        + [pltpu.VMEM((NARROW, ROWS), F32)] * 6
        + [
            pltpu.VMEM((2, NONE + 1, 3, NARROW, 2 * DOF), BF16),
            pltpu.VMEM((LAYER, 3, DOF, 8 * DOF), BF16),
            pltpu.VMEM((2, STAGED, SIDES, DOF, DOF), F32),
        ]
        + slots(2 * NARROW)
        + slots(3 * NARROW)
        + slots(NARROW)
        + [pltpu.VMEM((count * NARROW, K), F32) for count in (2, 3, 1)]
        + [pltpu.VMEM((K, K), F32)] * 5
        + [
            pltpu.SemaphoreType.DMA((2,)),
            pltpu.SemaphoreType.DMA((2, 2)),
            pltpu.SemaphoreType.DMA((2, 2)),
            pltpu.SemaphoreType.DMA((3, YS - 1)),
            pltpu.SemaphoreType.DMA((3, YS - 1)),
            pltpu.SemaphoreType.DMA((3, 3, 7)),
            pltpu.SemaphoreType.DMA((3, 3, 7)),
        ],
        compiler_params=pltpu.CompilerParams(
            collective_id=1, has_side_effects=True, vmem_limit_bytes=60 * 2**20
        ),
    )(index, start.T, mask, blocks)
    return basis.T, jnp.swapaxes(coefficients, 1, 2)


def solution(mesh):
    in_specs = (P("space", "blk"), P("space", None), P("space"), P("space", None, None, None))
    out_specs = (P("space", "blk"), P(None, None, "blk"))
    return jax.shard_map(local, mesh=mesh, in_specs=in_specs, out_specs=out_specs, check_vma=False)
```

```python
import jax
import jax.numpy as jnp
from jax import lax
from jax.experimental import pallas as pl
from jax.experimental.pallas import tpu as pltpu
from jax.sharding import PartitionSpec as P

LAYER = 64
DOF = 64
ROWS = LAYER * DOF
K = 128
CORES = 2
XS = 4
ZS = 8
YS = 4
SPACE = ZS * XS * CORES
NARROW = K // YS
SIDES = 7
PARTS = 4
PART = ROWS // PARTS
HALF = ROWS // 2
NONE = 3 * LAYER
WIDE = 32
SUB = 8
CHUNK = 512
STAGED = 16
MESH = pl.DeviceIdType.MESH
F32 = jnp.float32
BF16 = jnp.bfloat16


def dot(left, right, left_dim, right_dim):
    return lax.dot_general(
        left,
        right,
        (((left_dim,), (right_dim,)), ((), ())),
        precision=lax.Precision.HIGHEST,
        preferred_element_type=F32,
    )


def times(left, right):
    return dot(left, right, 1, 0)


def cross(left, right):
    return dot(left, right, 1, 1)


def split(value):
    first = value.astype(BF16)
    rest = value - first.astype(F32)
    second = rest.astype(BF16)
    return first, second, (rest - second.astype(F32)).astype(BF16)


def eliminate(gram, unit, first):
    shape = gram.shape
    row_id = lax.broadcasted_iota(jnp.int32, shape, 0)
    for sub in range(0, WIDE, SUB):
        columns = [
            jnp.broadcast_to(gram[:, first + sub + j : first + sub + j + 1], shape)
            for j in range(SUB)
        ]
        for j in range(SUB):
            k = sub + j
            scale = lax.rsqrt(jnp.broadcast_to(columns[j][k : k + 1], shape))
            pivot_gram = jnp.broadcast_to(gram[k : k + 1], shape) * scale
            pivot_unit = jnp.broadcast_to(unit[k : k + 1], shape) * scale
            below = jnp.where(row_id > k, columns[j], 0.0) * scale
            for other in range(j + 1, SUB):
                near = jnp.broadcast_to(columns[j][sub + other : sub + other + 1], shape)
                columns[other] = columns[other] - below * (near * scale)
            gram = jnp.where(row_id == k, pivot_gram, gram - below * pivot_gram)
            unit = jnp.where(row_id == k, pivot_unit, unit - below * pivot_unit)
    return gram, unit


def factor_rows(gram_ref, upper, inverse, first):
    row_id = lax.broadcasted_iota(jnp.int32, (WIDE, K), 0)
    col_id = lax.broadcasted_iota(jnp.int32, (WIDE, K), 1)
    rows = pl.ds(first, WIDE)
    gram = gram_ref[rows, :]
    unit = jnp.where(row_id + first == col_id, 1.0, 0.0)
    if first:
        above_gram = upper[pl.ds(0, first), :]
        above_unit = inverse[pl.ds(0, first), :]
        left = above_gram[:, first : first + WIDE]
        gram = gram - dot(left, above_gram, 0, 0)
        unit = unit - dot(left, above_unit, 0, 0)
    gram, unit = eliminate(gram, unit, first)
    upper[rows, :] = jnp.where(row_id + first <= col_id, gram, 0.0)
    inverse[rows, :] = unit


def factor_gram(gram_ref, upper, inverse):
    for first in range(0, K, WIDE):
        factor_rows(gram_ref, upper, inverse, first)


def prepare(staged, packed, base):
    def body(elem, carry):
        for pair in range(4):
            if pair < 3:
                right = staged[elem, 2 * pair + 1]
            else:
                right = jnp.zeros((DOF, DOF), F32)
            both = jnp.concatenate([staged[elem, 2 * pair], right], axis=1)
            for piece, value in enumerate(split(both)):
                packed[base + elem, piece, :, pair * 128 : (pair + 1) * 128] = value
        return carry

    lax.fori_loop(0, STAGED, body, 0, unroll=2)


def spread(source, elems, base, part):
    is_low = lax.broadcasted_iota(jnp.int32, (NARROW, 2 * DOF), 1) < DOF

    count = LAYER // 2 // PARTS

    def body(step, carry):
        pair = part * count + step
        straight = source[:, pl.ds(pl.multiple_of(pair * 128, 128), 128)]
        turned = pltpu.roll(straight, DOF, 1)
        for side, low, high in ((0, straight, turned), (1, turned, straight)):
            place = base + 2 * pair + side
            for piece, value in enumerate(split(jnp.where(is_low, low, 0.0))):
                elems[0, place, piece] = value
            for piece, value in enumerate(split(jnp.where(is_low, 0.0, high))):
                elems[1, place, piece] = value
        return carry

    lax.fori_loop(0, count, body, 0, unroll=2)


def solid(cavity, elem):
    return (1 - cavity[elem]).astype(F32)


def operate(faces, shift, cavity, elems, packed, out, own_rows, begin, end):
    def product(left, right):
        return lax.dot_general(
            left, right, (((1,), (1,)), ((), ())), preferred_element_type=F32
        )

    def one(elem):
        at = [LAYER + elem]
        for side in range(SIDES - 1):
            beside = faces[side, elem]
            at.append(jnp.where(beside < 0, NONE, jnp.clip(beside + shift, 0, NONE - 1)))
        pieces = []
        for piece in range(3):
            pairs = [
                elems[0, at[2 * pair], piece] + elems[1, at[2 * pair + 1], piece]
                for pair in range(3)
            ]
            pairs.append(elems[0, at[6], piece])
            pieces.append(jnp.concatenate(pairs, axis=1))
        three = product(jnp.concatenate(pieces, axis=0), packed[elem, 0])
        two = product(jnp.concatenate(pieces[:2], axis=0), packed[elem, 1])
        last = product(pieces[0], packed[elem, 2])
        small = three[2 * NARROW :] + two[NARROW:] + last
        value = three[:NARROW] + (three[NARROW : 2 * NARROW] + two[:NARROW] + small)
        return value * solid(cavity, elem)

    def body(pair, carry):
        cols = pl.ds(pl.multiple_of(pair * 128, 128), 128)
        out[own_rows, cols] = jnp.concatenate([one(2 * pair), one(2 * pair + 1)], axis=1)
        return carry

    lax.fori_loop(begin, end, body, 0, unroll=4)


def kernel(
    faces,
    cavity,
    start,
    blocks,
    basis_out,
    coef_out,
    basis,
    image,
    second,
    send_0,
    low_0,
    high_0,
    send_1,
    low_1,
    high_1,
    elems,
    packed,
    staged,
    near_0,
    far_0,
    done_0,
    near_1,
    far_1,
    done_1,
    near_2,
    far_2,
    done_2,
    near_3,
    far_3,
    done_3,
    part_0,
    part_1,
    part_2,
    part_3,
    gram,
    upper,
    inverse,
    alpha,
    flip,
    stage_sem,
    halo_send,
    halo_recv,
    rows_send,
    rows_recv,
    sums_send,
    sums_recv,
):
    space = lax.axis_index("space")
    blk = lax.axis_index("blk")
    core = lax.rem(space, CORES)
    spot = lax.rem(space, XS * CORES)
    plane = space // (XS * CORES)
    plane_base = plane * (XS * CORES)
    quad = blk * CORES + core
    right = lax.rem(blk + 1, YS)
    left = lax.rem(blk + YS - 1, YS)
    shift = LAYER - space * LAYER
    own_rows = pl.ds(pl.multiple_of(blk * NARROW, NARROW), NARROW)
    right_rows = pl.ds(pl.multiple_of(right * NARROW, NARROW), NARROW)
    left_rows = pl.ds(pl.multiple_of(left * NARROW, NARROW), NARROW)
    above = (lax.rem(space + 1, SPACE), blk)
    below = (lax.rem(space + SPACE - 1, SPACE), blk)
    near_ids = [lax.rem(spot + step, 8) for step in range(1, 8)]
    near_devices = [(plane_base + near, blk) for near in near_ids]
    far_devices = [(lax.rem(plane + step, 8) * 8 + spot, blk) for step in range(1, 8)]
    quads = [lax.rem(quad + step, 8) for step in range(1, 8)]
    done_devices = [(space - core + lax.rem(q, CORES), q // CORES) for q in quads]

    def stage_copy(part):
        return pltpu.make_async_copy(
            blocks.at[pl.ds(part * STAGED, STAGED)], staged.at[part % 2], stage_sem.at[part % 2]
        )

    stage_copy(0).start()
    stage_copy(1).start()
    barrier = pltpu.get_barrier_semaphore()
    for device in near_devices + far_devices + done_devices + [above, below]:
        pl.semaphore_signal(barrier, inc=1, device_id=device, device_id_type=MESH)

    def masked(array, rows, send, part):
        is_low = lax.broadcasted_iota(jnp.int32, (NARROW, 2 * DOF), 1) < DOF
        count = LAYER // 2 // PARTS
        for step in range(count):
            pair = part * count + step
            cols = pl.ds(pl.multiple_of(pair * 128, 128), 128)
            weight = jnp.where(is_low, solid(cavity, 2 * pair), solid(cavity, 2 * pair + 1))
            send[:, cols] = array[rows, cols] * weight

    def halo_copies(call, part, send, low, high):
        cols = pl.ds(pl.multiple_of(part * PART, PART), PART)
        return [
            pltpu.make_async_remote_copy(
                src_ref=send.at[:, cols],
                dst_ref=target.at[:, cols],
                send_sem=halo_send.at[call, way, part],
                recv_sem=halo_recv.at[call, way, part],
                device_id=device,
                device_id_type=MESH,
            )
            for way, target, device in ((0, low, above), (1, high, below))
        ]

    def rows_copy(call, slot, array, rows, half, target):
        place = array.at[rows, pl.ds(half * HALF, HALF)]
        return pltpu.make_async_remote_copy(
            src_ref=place,
            dst_ref=place,
            send_sem=rows_send.at[call, slot],
            recv_sem=rows_recv.at[call, slot],
            device_id=(space, target),
            device_id_type=MESH,
        )

    def gather(call, array):
        copies = [
            rows_copy(call, 0, array, own_rows, 0, right),
            rows_copy(call, 1, array, own_rows, 1, left),
            rows_copy(call, 2, array, own_rows, 1, right),
            rows_copy(call, 3, array, own_rows, 0, left),
        ]
        for copy in copies:
            copy.start()
        return copies

    def relay(call, array, copies):
        copies[0].wait_recv()
        onward = rows_copy(call, 4, array, left_rows, 0, right)
        onward.start()
        copies[1].wait_recv()
        back = rows_copy(call, 5, array, right_rows, 1, left)
        back.start()
        return copies + [onward, back]

    def gathered(copies):
        copies[0].wait_send()
        copies[1].wait_send()
        for copy in copies[2:]:
            copy.wait()

    def wait(copies):
        for copy in copies:
            copy.wait()

    def exchange(call, stage, sources, slots, mine, devices):
        copies = []
        for step in range(7):
            copy = pltpu.make_async_remote_copy(
                src_ref=sources[step],
                dst_ref=slots.at[mine],
                send_sem=sums_send.at[call, stage, step],
                recv_sem=sums_recv.at[call, stage, step],
                device_id=devices[step],
                device_id_type=MESH,
            )
            copy.start()
            copies.append(copy)
        return copies

    def total(slots):
        value = slots[0]
        for slot in range(1, 8):
            value = value + slots[slot]
        return value

    def reduce_near(call, part, near):
        half = part.shape[0] // CORES
        sources = [
            part.at[pl.ds(pl.multiple_of(lax.rem(spot_id, CORES) * half, 8), half)]
            for spot_id in near_ids
        ]
        copies = exchange(call, 0, sources, near, spot, near_devices)
        near[spot] = part[pl.ds(pl.multiple_of(core * half, 8), half), :]
        return copies

    def reduce_far(call, copies, near, far):
        wait(copies)
        far[plane] = total(near)
        return exchange(call, 1, [far.at[plane]] * 7, far, plane, far_devices)

    def reduce_done(call, copies, far, done):
        wait(copies)
        done[quad] = total(far)
        return exchange(call, 2, [done.at[quad]] * 7, done, quad, done_devices)

    def square(done, which):
        rows = []
        for member in range(YS):
            panel = jnp.concatenate([done[2 * member], done[2 * member + 1]], axis=0)
            rows.append(panel[which * NARROW : (which + 1) * NARROW])
        return jnp.concatenate(rows, axis=0)

    def over_chunks(body, init):
        def step(chunk, carry):
            return body(pl.ds(pl.multiple_of(chunk * CHUNK, CHUNK), CHUNK), carry)

        return lax.fori_loop(0, ROWS // CHUNK, step, init)

    def over_parts(body):
        def step(part, carry):
            body(part)
            return carry

        lax.fori_loop(0, PARTS, step, 0)

    def keep_upper(which):
        flip[...] = upper[...].T
        coef_out[which] = flip[own_rows, :]

    def receive(call, send, low, high):
        def body(part):
            for copy in halo_copies(call, part, send, low, high):
                copy.wait()
            spread(low, elems, 0, part)
            spread(high, elems, 2 * LAYER, part)

        over_parts(body)

    def apply(out, begin, end):
        operate(faces, shift, cavity, elems, packed, out, own_rows, begin, end)

    basis[own_rows, :] = start[...]
    over_parts(lambda part: masked(start, slice(None), send_0, part))
    pl.semaphore_wait(barrier, 23)

    def start_halo(part):
        for copy in halo_copies(0, part, send_0, low_0, high_0):
            copy.start()

    over_parts(start_halo)
    start_copies = gather(0, basis)
    for part in range(LAYER // STAGED):
        stage_copy(part).wait()
        prepare(staged.at[part % 2], packed, part * STAGED)
        if part + 2 < LAYER // STAGED:
            stage_copy(part + 2).start()
    for which in range(2):
        for piece in range(3):
            elems[which, NONE, piece] = jnp.zeros((NARROW, 2 * DOF), BF16)
    over_parts(lambda part: spread(send_0, elems, LAYER, part))
    start_copies = relay(0, basis, start_copies)
    receive(0, send_0, low_0, high_0)
    apply(image, 0, LAYER // 2)
    image_copies = gather(1, image)
    gathered(start_copies)

    def start_products(cols, carry):
        own = jnp.concatenate([basis[own_rows, cols], image[own_rows, cols]], axis=0)
        return carry + cross(own, basis[:, cols])

    part_0[...] = over_chunks(start_products, jnp.zeros(part_0.shape, F32))
    sums = reduce_near(0, part_0, near_0)
    sums = reduce_far(0, sums, near_0, far_0)
    image_copies = relay(1, image, image_copies)
    wait(reduce_done(0, sums, far_0, done_0))
    gram[...] = square(done_0, 0)
    factor_gram(gram, upper, inverse)
    alpha[...] = cross(times(inverse[...], square(done_0, 1)), inverse[...])
    gathered(image_copies)

    def first_residue(part):
        for side in range(PART // CHUNK):
            cols = pl.ds(pl.multiple_of(part * PART + side * CHUNK, CHUNK), CHUNK)
            vectors = times(inverse[...], basis[:, cols])
            basis[:, cols] = vectors
            image[:, cols] = times(inverse[...], image[:, cols]) - times(alpha[...], vectors)
        masked(image, own_rows, send_1, part)
        for copy in halo_copies(1, part, send_1, low_1, high_1):
            copy.start()

    over_parts(first_residue)

    def residue_products(cols, carry):
        own = image[own_rows, cols]
        return carry[0] + cross(own, image[:, cols]), carry[1] + cross(own, basis[:, cols])

    empty = jnp.zeros((NARROW, K), F32)
    products = over_chunks(residue_products, (empty, empty))
    part_1[pl.ds(0, NARROW), :] = products[0]
    part_1[pl.ds(NARROW, NARROW), :] = products[1]
    sums = reduce_near(1, part_1, near_1)
    coef_out[1] = alpha[own_rows, :]
    keep_upper(0)
    over_parts(lambda part: spread(send_1, elems, LAYER, part))
    receive(1, send_1, low_1, high_1)
    sums = reduce_far(1, sums, near_1, far_1)
    apply(second, 0, LAYER // 2)
    second_copies = gather(2, second)
    sums = reduce_done(1, sums, far_1, done_1)

    def image_products(cols, carry):
        return carry + cross(second[own_rows, cols], image[:, cols])

    part_2[...] = over_chunks(image_products, empty)
    inner_sums = reduce_near(2, part_2, near_2)
    wait(sums)
    gram[...] = square(done_1, 0)
    for first in range(0, K, WIDE):
        factor_rows(gram, upper, inverse, first)
        if first == WIDE:
            inner_sums = reduce_far(2, inner_sums, near_2, far_2)
    second_copies = relay(2, second, second_copies)
    skew = cross(upper[...], times(inverse[...], square(done_1, 1)))
    inner_sums = reduce_done(2, inner_sums, far_2, done_2)

    def second_basis(cols, carry):
        image[:, cols] = times(inverse[...], image[:, cols])
        return carry

    over_chunks(second_basis, 0)
    gathered(second_copies)

    def second_image(cols, carry):
        value = times(inverse[...], second[:, cols])
        second[:, cols] = value - times(upper[...], basis[:, cols])
        return carry

    over_chunks(second_image, 0)
    keep_upper(2)
    wait(inner_sums)
    inner = cross(times(inverse[...], square(done_2, 0)), inverse[...])
    alpha[...] = inner - skew

    def second_residue(cols, carry):
        value = second[:, cols] - times(alpha[...], image[:, cols])
        second[:, cols] = value
        return carry + cross(second[own_rows, cols], value)

    part_3[...] = over_chunks(second_residue, empty)
    sums = reduce_near(3, part_3, near_3)
    coef_out[3] = alpha[own_rows, :]
    sums = reduce_far(3, sums, near_3, far_3)
    wait(reduce_done(3, sums, far_3, done_3))
    gram[...] = square(done_3, 0)
    factor_gram(gram, upper, inverse)
    keep_upper(4)

    def last_basis(cols, carry):
        basis_out[:, cols] = times(inverse[own_rows, :], second[:, cols])
        return carry

    over_chunks(last_basis, 0)


def local(start, faces, cavity, blocks):
    smem = pl.BlockSpec(memory_space=pltpu.SMEM)
    vmem = pl.BlockSpec(memory_space=pltpu.VMEM)

    def slots(rows):
        return [pltpu.VMEM((8, rows // CORES, K), F32)] * 3

    basis, coefficients = pl.pallas_call(
        kernel,
        out_shape=(
            jax.ShapeDtypeStruct((NARROW, ROWS), F32),
            jax.ShapeDtypeStruct((5, NARROW, K), F32),
        ),
        in_specs=[
            smem,
            smem,
            vmem,
            pl.BlockSpec(memory_space=pl.ANY),
        ],
        out_specs=(vmem, vmem),
        scratch_shapes=[pltpu.VMEM((K, ROWS), F32)] * 3
        + [pltpu.VMEM((NARROW, ROWS), F32)] * 6
        + [
            pltpu.VMEM((2, NONE + 1, 3, NARROW, 2 * DOF), BF16),
            pltpu.VMEM((LAYER, 3, DOF, 8 * DOF), BF16),
            pltpu.VMEM((2, STAGED, SIDES, DOF, DOF), F32),
        ]
        + slots(2 * NARROW)
        + slots(2 * NARROW)
        + slots(NARROW)
        + slots(NARROW)
        + [pltpu.VMEM((count * NARROW, K), F32) for count in (2, 2, 1, 1)]
        + [pltpu.VMEM((K, K), F32)] * 5
        + [
            pltpu.SemaphoreType.DMA((2,)),
            pltpu.SemaphoreType.DMA((2, 2, PARTS)),
            pltpu.SemaphoreType.DMA((2, 2, PARTS)),
            pltpu.SemaphoreType.DMA((3, 6)),
            pltpu.SemaphoreType.DMA((3, 6)),
            pltpu.SemaphoreType.DMA((4, 3, 7)),
            pltpu.SemaphoreType.DMA((4, 3, 7)),
        ],
        compiler_params=pltpu.CompilerParams(
            collective_id=1, has_side_effects=True, vmem_limit_bytes=60 * 2**20
        ),
    )(faces.T, cavity, start.T, blocks)
    return basis.T, jnp.swapaxes(coefficients, 1, 2)


def solution(mesh):
    in_specs = (P("space", "blk"), P("space", None), P("space"), P("space", None, None, None))
    out_specs = (P("space", "blk"), P(None, None, "blk"))
    return jax.shard_map(local, mesh=mesh, in_specs=in_specs, out_specs=out_specs, check_vma=False)
```

```python
import jax
import jax.numpy as jnp
from jax import lax
from jax.experimental import pallas as pl
from jax.experimental.pallas import tpu as pltpu
from jax.sharding import PartitionSpec as P

LAYER = 64
DOF = 64
ROWS = LAYER * DOF
K = 128
CORES = 2
XS = 4
ZS = 8
YS = 4
SPACE = ZS * XS * CORES
NARROW = K // YS
SIDES = 7
PARTS = 4
PART = ROWS // PARTS
HALF = ROWS // 2
NONE = 3 * LAYER
WIDE = 32
SUB = 8
CHUNK = 512
STAGED = 16
MESH = pl.DeviceIdType.MESH
F32 = jnp.float32
BF16 = jnp.bfloat16


def dot(left, right, left_dim, right_dim):
    return lax.dot_general(
        left,
        right,
        (((left_dim,), (right_dim,)), ((), ())),
        precision=lax.Precision.HIGHEST,
        preferred_element_type=F32,
    )


def times(left, right):
    return dot(left, right, 1, 0)


def cross(left, right):
    return dot(left, right, 1, 1)


def split(value):
    first = value.astype(BF16)
    rest = value - first.astype(F32)
    second = rest.astype(BF16)
    return first, second, (rest - second.astype(F32)).astype(BF16)


def eliminate(gram, unit, first):
    shape = gram.shape
    row_id = lax.broadcasted_iota(jnp.int32, shape, 0)
    for sub in range(0, WIDE, SUB):
        columns = [
            jnp.broadcast_to(gram[:, first + sub + j : first + sub + j + 1], shape)
            for j in range(SUB)
        ]
        for j in range(SUB):
            k = sub + j
            scale = lax.rsqrt(jnp.broadcast_to(columns[j][k : k + 1], shape))
            pivot_gram = jnp.broadcast_to(gram[k : k + 1], shape) * scale
            pivot_unit = jnp.broadcast_to(unit[k : k + 1], shape) * scale
            below = jnp.where(row_id > k, columns[j], 0.0) * scale
            for other in range(j + 1, SUB):
                near = jnp.broadcast_to(columns[j][sub + other : sub + other + 1], shape)
                columns[other] = columns[other] - below * (near * scale)
            gram = jnp.where(row_id == k, pivot_gram, gram - below * pivot_gram)
            unit = jnp.where(row_id == k, pivot_unit, unit - below * pivot_unit)
    return gram, unit


def factor_rows(gram_ref, upper, inverse, first):
    row_id = lax.broadcasted_iota(jnp.int32, (WIDE, K), 0)
    col_id = lax.broadcasted_iota(jnp.int32, (WIDE, K), 1)
    rows = pl.ds(first, WIDE)
    gram = gram_ref[rows, :]
    unit = jnp.where(row_id + first == col_id, 1.0, 0.0)
    if first:
        above_gram = upper[pl.ds(0, first), :]
        above_unit = inverse[pl.ds(0, first), :]
        left = above_gram[:, first : first + WIDE]
        gram = gram - dot(left, above_gram, 0, 0)
        unit = unit - dot(left, above_unit, 0, 0)
    gram, unit = eliminate(gram, unit, first)
    upper[rows, :] = jnp.where(row_id + first <= col_id, gram, 0.0)
    inverse[rows, :] = unit


def factor_gram(gram_ref, upper, inverse):
    for first in range(0, K, WIDE):
        factor_rows(gram_ref, upper, inverse, first)


def prepare(staged, packed, base):
    def body(elem, carry):
        for pair in range(4):
            if pair < 3:
                right = staged[elem, 2 * pair + 1]
            else:
                right = jnp.zeros((DOF, DOF), F32)
            both = jnp.concatenate([staged[elem, 2 * pair], right], axis=1)
            for piece, value in enumerate(split(both)):
                packed[base + elem, piece, :, pair * 128 : (pair + 1) * 128] = value
        return carry

    lax.fori_loop(0, STAGED, body, 0, unroll=2)


def spread(source, elems, base, part):
    is_low = lax.broadcasted_iota(jnp.int32, (NARROW, 2 * DOF), 1) < DOF
    count = LAYER // 2 // PARTS

    def body(step, carry):
        pair = part * count + step
        straight = source[:, pl.ds(pl.multiple_of(pair * 128, 128), 128)]
        turned = pltpu.roll(straight, DOF, 1)
        for side, low, high in ((0, straight, turned), (1, turned, straight)):
            place = base + 2 * pair + side
            for piece, value in enumerate(split(jnp.where(is_low, low, 0.0))):
                elems[0, place, piece] = value
            for piece, value in enumerate(split(jnp.where(is_low, 0.0, high))):
                elems[1, place, piece] = value
        return carry

    lax.fori_loop(0, count, body, 0, unroll=8)


def solid(cavity, elem):
    return (1 - cavity[elem]).astype(F32)


def operate(faces, shift, cavity, elems, packed, out, own_rows, begin, end):
    def product(left, right):
        return lax.dot_general(
            left, right, (((1,), (1,)), ((), ())), preferred_element_type=F32
        )

    def one(elem):
        at = [LAYER + elem]
        for side in range(SIDES - 1):
            beside = faces[side, elem]
            at.append(jnp.where(beside < 0, NONE, jnp.clip(beside + shift, 0, NONE - 1)))
        pieces = []
        for piece in range(3):
            pairs = [
                elems[0, at[2 * pair], piece] + elems[1, at[2 * pair + 1], piece]
                for pair in range(3)
            ]
            pairs.append(elems[0, at[6], piece])
            pieces.append(jnp.concatenate(pairs, axis=1))
        three = product(jnp.concatenate(pieces, axis=0), packed[elem, 0])
        two = product(jnp.concatenate(pieces[:2], axis=0), packed[elem, 1])
        last = product(pieces[0], packed[elem, 2])
        small = three[2 * NARROW :] + two[NARROW:] + last
        value = three[:NARROW] + (three[NARROW : 2 * NARROW] + two[:NARROW] + small)
        return value * solid(cavity, elem)

    def body(pair, carry):
        cols = pl.ds(pl.multiple_of(pair * 128, 128), 128)
        out[own_rows, cols] = jnp.concatenate([one(2 * pair), one(2 * pair + 1)], axis=1)
        return carry

    lax.fori_loop(begin, end, body, 0, unroll=4)


def kernel(
    faces,
    cavity,
    start,
    blocks,
    basis_out,
    coef_out,
    basis,
    image,
    second,
    send_0,
    low_0,
    high_0,
    send_1,
    low_1,
    high_1,
    elems,
    packed,
    staged,
    near_0,
    far_0,
    done_0,
    near_1,
    far_1,
    done_1,
    near_2,
    far_2,
    done_2,
    near_3,
    far_3,
    done_3,
    part_0,
    part_1,
    part_2,
    part_3,
    gram,
    upper,
    inverse,
    alpha,
    flip,
    update,
    stage_sem,
    halo_send,
    halo_recv,
    rows_send,
    rows_recv,
    sums_send,
    sums_recv,
):
    space = lax.axis_index("space")
    blk = lax.axis_index("blk")
    core = lax.rem(space, CORES)
    spot = lax.rem(space, XS * CORES)
    plane = space // (XS * CORES)
    plane_base = plane * (XS * CORES)
    quad = blk * CORES + core
    right = lax.rem(blk + 1, YS)
    left = lax.rem(blk + YS - 1, YS)
    shift = LAYER - space * LAYER
    own_rows = pl.ds(pl.multiple_of(blk * NARROW, NARROW), NARROW)
    right_rows = pl.ds(pl.multiple_of(right * NARROW, NARROW), NARROW)
    left_rows = pl.ds(pl.multiple_of(left * NARROW, NARROW), NARROW)
    above = (lax.rem(space + 1, SPACE), blk)
    below = (lax.rem(space + SPACE - 1, SPACE), blk)
    near_ids = [lax.rem(spot + step, 8) for step in range(1, 8)]
    near_devices = [(plane_base + near, blk) for near in near_ids]
    far_devices = [(lax.rem(plane + step, 8) * 8 + spot, blk) for step in range(1, 8)]
    quads = [lax.rem(quad + step, 8) for step in range(1, 8)]
    done_devices = [(space - core + lax.rem(q, CORES), q // CORES) for q in quads]

    def stage_copy(part):
        return pltpu.make_async_copy(
            blocks.at[pl.ds(part * STAGED, STAGED)], staged.at[part % 2], stage_sem.at[part % 2]
        )

    stage_copy(0).start()
    stage_copy(1).start()
    barrier = pltpu.get_barrier_semaphore()
    for device in near_devices + far_devices + done_devices + [above, below]:
        pl.semaphore_signal(barrier, inc=1, device_id=device, device_id_type=MESH)

    def masked(array, rows, send, part):
        is_low = lax.broadcasted_iota(jnp.int32, (NARROW, 2 * DOF), 1) < DOF
        count = LAYER // 2 // PARTS
        for step in range(count):
            pair = part * count + step
            cols = pl.ds(pl.multiple_of(pair * 128, 128), 128)
            weight = jnp.where(is_low, solid(cavity, 2 * pair), solid(cavity, 2 * pair + 1))
            send[:, cols] = array[rows, cols] * weight

    def halo_copies(call, part, send, low, high):
        cols = pl.ds(pl.multiple_of(part * PART, PART), PART)
        return [
            pltpu.make_async_remote_copy(
                src_ref=send.at[:, cols],
                dst_ref=target.at[:, cols],
                send_sem=halo_send.at[call, way, part],
                recv_sem=halo_recv.at[call, way, part],
                device_id=device,
                device_id_type=MESH,
            )
            for way, target, device in ((0, low, above), (1, high, below))
        ]

    def rows_copy(call, slot, array, rows, half, target):
        place = array.at[rows, pl.ds(half * HALF, HALF)]
        return pltpu.make_async_remote_copy(
            src_ref=place,
            dst_ref=place,
            send_sem=rows_send.at[call, slot],
            recv_sem=rows_recv.at[call, slot],
            device_id=(space, target),
            device_id_type=MESH,
        )

    def gather(call, array, half):
        copies = [
            rows_copy(call, 2 * half, array, own_rows, half, (right, left)[half]),
            rows_copy(call, 2 * half + 1, array, own_rows, half, (left, right)[half]),
        ]
        for copy in copies:
            copy.start()
        return copies

    def relay(call, array, copies):
        copies[0].wait_recv()
        onward = rows_copy(call, 4, array, left_rows, 0, right)
        onward.start()
        copies[2].wait_recv()
        back = rows_copy(call, 5, array, right_rows, 1, left)
        back.start()
        return copies + [onward, back]

    def gathered(copies):
        for slot, copy in enumerate(copies):
            if slot not in (0, 2):
                copy.wait_recv()
        for copy in copies:
            copy.wait_send()

    sent = []

    def wait(copies):
        for copy in copies:
            copy.wait_recv()
        sent.extend(copies)

    def exchange(call, stage, sources, slots, mine, devices):
        copies = []
        for step in range(7):
            copy = pltpu.make_async_remote_copy(
                src_ref=sources[step],
                dst_ref=slots.at[mine],
                send_sem=sums_send.at[call, stage, step],
                recv_sem=sums_recv.at[call, stage, step],
                device_id=devices[step],
                device_id_type=MESH,
            )
            copy.start()
            copies.append(copy)
        return copies

    def total(slots):
        value = slots[0]
        for slot in range(1, 8):
            value = value + slots[slot]
        return value

    def reduce_near(call, part, near):
        half = part.shape[0] // CORES
        sources = [
            part.at[pl.ds(pl.multiple_of(lax.rem(spot_id, CORES) * half, 8), half)]
            for spot_id in near_ids
        ]
        copies = exchange(call, 0, sources, near, spot, near_devices)
        near[spot] = part[pl.ds(pl.multiple_of(core * half, 8), half), :]
        return copies

    def reduce_far(call, copies, near, far):
        wait(copies)
        far[plane] = total(near)
        return exchange(call, 1, [far.at[plane]] * 7, far, plane, far_devices)

    def reduce_done(call, copies, far, done):
        wait(copies)
        done[quad] = total(far)
        return exchange(call, 2, [done.at[quad]] * 7, done, quad, done_devices)

    def square(done, which):
        rows = []
        for member in range(YS):
            panel = jnp.concatenate([done[2 * member], done[2 * member + 1]], axis=0)
            rows.append(panel[which * NARROW : (which + 1) * NARROW])
        return jnp.concatenate(rows, axis=0)

    def over_chunks(body, init):
        def step(chunk, carry):
            return body(pl.ds(pl.multiple_of(chunk * CHUNK, CHUNK), CHUNK), carry)

        return lax.fori_loop(0, ROWS // CHUNK, step, init)

    def over_parts(body):
        def step(part, carry):
            body(part)
            return carry

        lax.fori_loop(0, PARTS, step, 0)

    def keep_upper(which):
        flip[...] = upper[...].T
        coef_out[which] = flip[own_rows, :]

    def receive(call, send, low, high, first, count):
        def body(step, carry):
            part = first + step
            for copy in halo_copies(call, part, send, low, high):
                copy.wait()
            spread(low, elems, 0, part)
            spread(high, elems, 2 * LAYER, part)
            return carry

        lax.fori_loop(0, count, body, 0)

    def apply(out, begin, end):
        operate(faces, shift, cavity, elems, packed, out, own_rows, begin, end)

    basis[own_rows, :] = start[...]
    over_parts(lambda part: masked(start, slice(None), send_0, part))
    pl.semaphore_wait(barrier, 23)

    def start_halo(part):
        for copy in halo_copies(0, part, send_0, low_0, high_0):
            copy.start()

    over_parts(start_halo)
    start_copies = gather(0, basis, 0) + gather(0, basis, 1)
    for part in range(LAYER // STAGED):
        stage_copy(part).wait()
        prepare(staged.at[part % 2], packed, part * STAGED)
        if part + 2 < LAYER // STAGED:
            stage_copy(part + 2).start()
    for which in range(2):
        for piece in range(3):
            elems[which, NONE, piece] = jnp.zeros((NARROW, 2 * DOF), BF16)
    over_parts(lambda part: spread(send_0, elems, LAYER, part))
    start_copies = relay(0, basis, start_copies)
    receive(0, send_0, low_0, high_0, 0, PARTS)
    apply(image, 0, LAYER // 4)
    image_copies = gather(1, image, 0)
    apply(image, LAYER // 4, LAYER // 2)
    image_copies += gather(1, image, 1)
    gathered(start_copies)

    def start_products(cols, carry):
        own = jnp.concatenate([basis[own_rows, cols], image[own_rows, cols]], axis=0)
        return carry + cross(own, basis[:, cols])

    part_0[...] = over_chunks(start_products, jnp.zeros(part_0.shape, F32))
    sums = reduce_near(0, part_0, near_0)
    sums = reduce_far(0, sums, near_0, far_0)
    image_copies = relay(1, image, image_copies)
    wait(reduce_done(0, sums, far_0, done_0))
    gram[...] = square(done_0, 0)
    factor_gram(gram, upper, inverse)
    alpha[...] = cross(times(inverse[...], square(done_0, 1)), inverse[...])
    update[:, pl.ds(0, K)] = inverse[...]
    update[:, pl.ds(K, K)] = -times(alpha[...], inverse[...])
    gathered(image_copies)

    def first_residue(part):
        for side in range(PART // CHUNK):
            cols = pl.ds(pl.multiple_of(part * PART + side * CHUNK, CHUNK), CHUNK)
            both = jnp.concatenate([image[:, cols], basis[:, cols]], axis=0)
            image[:, cols] = times(update[...], both)
        masked(image, own_rows, send_1, part)
        for copy in halo_copies(1, part, send_1, low_1, high_1):
            copy.start()

    over_parts(first_residue)

    def residue_products(cols, carry):
        own = image[own_rows, cols]
        vectors = times(inverse[...], basis[:, cols])
        basis[:, cols] = vectors
        return carry[0] + cross(own, image[:, cols]), carry[1] + cross(own, vectors)

    empty = jnp.zeros((NARROW, K), F32)
    products = over_chunks(residue_products, (empty, empty))
    part_1[pl.ds(0, NARROW), :] = products[0]
    part_1[pl.ds(NARROW, NARROW), :] = products[1]
    sums = reduce_near(1, part_1, near_1)
    coef_out[1] = alpha[own_rows, :]
    keep_upper(0)
    over_parts(lambda part: spread(send_1, elems, LAYER, part))
    receive(1, send_1, low_1, high_1, 0, 3)
    sums = reduce_far(1, sums, near_1, far_1)
    receive(1, send_1, low_1, high_1, 3, 1)
    apply(second, 0, LAYER // 4)
    second_copies = gather(2, second, 0)
    sums = reduce_done(1, sums, far_1, done_1)
    apply(second, LAYER // 4, LAYER // 2)
    second_copies += gather(2, second, 1)

    def image_products(cols, carry):
        return carry + cross(second[own_rows, cols], image[:, cols])

    part_2[...] = over_chunks(image_products, empty)
    inner_sums = reduce_near(2, part_2, near_2)
    wait(sums)
    gram[...] = square(done_1, 0)
    for first in range(0, K, WIDE):
        factor_rows(gram, upper, inverse, first)
        if first == WIDE:
            inner_sums = reduce_far(2, inner_sums, near_2, far_2)
    second_copies = relay(2, second, second_copies)
    skew = cross(upper[...], times(inverse[...], square(done_1, 1)))
    inner_sums = reduce_done(2, inner_sums, far_2, done_2)
    update[:, pl.ds(0, K)] = inverse[...]

    def second_basis(cols, carry):
        image[:, cols] = times(inverse[...], image[:, cols])
        basis[:, cols] = times(upper[...], basis[:, cols])
        return carry

    over_chunks(second_basis, 0)
    keep_upper(2)
    wait(inner_sums)
    inner = cross(times(inverse[...], square(done_2, 0)), inverse[...])
    alpha[...] = inner - skew
    update[:, pl.ds(K, K)] = -alpha[...]
    gathered(second_copies)

    def second_residue(cols, carry):
        both = jnp.concatenate([second[:, cols], image[:, cols]], axis=0)
        value = times(update[...], both) - basis[:, cols]
        second[:, cols] = value
        return carry + cross(second[own_rows, cols], value)

    part_3[...] = over_chunks(second_residue, empty)
    sums = reduce_near(3, part_3, near_3)
    coef_out[3] = alpha[own_rows, :]
    sums = reduce_far(3, sums, near_3, far_3)
    wait(reduce_done(3, sums, far_3, done_3))
    gram[...] = square(done_3, 0)
    factor_gram(gram, upper, inverse)
    keep_upper(4)

    def last_basis(cols, carry):
        basis_out[:, cols] = times(inverse[own_rows, :], second[:, cols])
        return carry

    over_chunks(last_basis, 0)
    for copy in sent:
        copy.wait_send()


def local(start, faces, cavity, blocks):
    smem = pl.BlockSpec(memory_space=pltpu.SMEM)
    vmem = pl.BlockSpec(memory_space=pltpu.VMEM)

    def slots(rows):
        return [pltpu.VMEM((8, rows // CORES, K), F32)] * 3

    basis, coefficients = pl.pallas_call(
        kernel,
        out_shape=(
            jax.ShapeDtypeStruct((NARROW, ROWS), F32),
            jax.ShapeDtypeStruct((5, NARROW, K), F32),
        ),
        in_specs=[
            smem,
            smem,
            vmem,
            pl.BlockSpec(memory_space=pl.ANY),
        ],
        out_specs=(vmem, vmem),
        scratch_shapes=[pltpu.VMEM((K, ROWS), F32)] * 3
        + [pltpu.VMEM((NARROW, ROWS), F32)] * 6
        + [
            pltpu.VMEM((2, NONE + 1, 3, NARROW, 2 * DOF), BF16),
            pltpu.VMEM((LAYER, 3, DOF, 8 * DOF), BF16),
            pltpu.VMEM((2, STAGED, SIDES, DOF, DOF), F32),
        ]
        + slots(2 * NARROW)
        + slots(2 * NARROW)
        + slots(NARROW)
        + slots(NARROW)
        + [pltpu.VMEM((count * NARROW, K), F32) for count in (2, 2, 1, 1)]
        + [pltpu.VMEM((K, K), F32)] * 5
        + [pltpu.VMEM((K, 2 * K), F32)]
        + [
            pltpu.SemaphoreType.DMA((2,)),
            pltpu.SemaphoreType.DMA((2, 2, PARTS)),
            pltpu.SemaphoreType.DMA((2, 2, PARTS)),
            pltpu.SemaphoreType.DMA((3, 6)),
            pltpu.SemaphoreType.DMA((3, 6)),
            pltpu.SemaphoreType.DMA((4, 3, 7)),
            pltpu.SemaphoreType.DMA((4, 3, 7)),
        ],
        compiler_params=pltpu.CompilerParams(
            collective_id=1, has_side_effects=True, vmem_limit_bytes=60 * 2**20
        ),
    )(faces.T, cavity, start.T, blocks)
    return basis.T, jnp.swapaxes(coefficients, 1, 2)


def solution(mesh):
    in_specs = (P("space", "blk"), P("space", None), P("space"), P("space", None, None, None))
    out_specs = (P("space", "blk"), P(None, None, "blk"))
    return jax.shard_map(local, mesh=mesh, in_specs=in_specs, out_specs=out_specs, check_vma=False)
```

```python
import jax
import jax.numpy as jnp
from jax import lax
from jax.experimental import pallas as pl
from jax.experimental.pallas import tpu as pltpu
from jax.sharding import PartitionSpec as P

LAYER = 64
DOF = 64
ROWS = LAYER * DOF
K = 128
CORES = 2
XS = 4
ZS = 8
YS = 4
SPACE = ZS * XS * CORES
NARROW = K // YS
SIDES = 7
PARTS = 4
PART = ROWS // PARTS
HALF = ROWS // 2
NONE = 3 * LAYER
WIDE = 32
SUB = 16
CHUNK = 512
STAGED = 16
MESH = pl.DeviceIdType.MESH
F32 = jnp.float32
BF16 = jnp.bfloat16


def dot(left, right, left_dim, right_dim):
    return lax.dot_general(
        left,
        right,
        (((left_dim,), (right_dim,)), ((), ())),
        precision=lax.Precision.HIGHEST,
        preferred_element_type=F32,
    )


def times(left, right):
    return dot(left, right, 1, 0)


def cross(left, right):
    return dot(left, right, 1, 1)


def split(value):
    first = value.astype(BF16)
    rest = value - first.astype(F32)
    second = rest.astype(BF16)
    return first, second, (rest - second.astype(F32)).astype(BF16)


def eliminate(gram, unit, first):
    shape = gram.shape
    row_id = lax.broadcasted_iota(jnp.int32, shape, 0)
    for sub in range(0, WIDE, SUB):
        columns = [
            jnp.broadcast_to(gram[:, first + sub + j : first + sub + j + 1], shape)
            for j in range(SUB)
        ]
        for j in range(SUB):
            k = sub + j
            scale = lax.rsqrt(jnp.broadcast_to(columns[j][k : k + 1], shape))
            pivot_gram = jnp.broadcast_to(gram[k : k + 1], shape) * scale
            pivot_unit = jnp.broadcast_to(unit[k : k + 1], shape) * scale
            below = jnp.where(row_id > k, columns[j], 0.0) * scale
            for other in range(j + 1, SUB):
                near = jnp.broadcast_to(columns[j][sub + other : sub + other + 1], shape)
                columns[other] = columns[other] - below * (near * scale)
            gram = jnp.where(row_id == k, pivot_gram, gram - below * pivot_gram)
            unit = jnp.where(row_id == k, pivot_unit, unit - below * pivot_unit)
    return gram, unit


def factor_rows(gram_ref, upper, inverse, first):
    row_id = lax.broadcasted_iota(jnp.int32, (WIDE, K), 0)
    col_id = lax.broadcasted_iota(jnp.int32, (WIDE, K), 1)
    rows = pl.ds(first, WIDE)
    gram = gram_ref[rows, :]
    unit = jnp.where(row_id + first == col_id, 1.0, 0.0)
    if first:
        above_gram = upper[pl.ds(0, first), :]
        above_unit = inverse[pl.ds(0, first), :]
        left = above_gram[:, first : first + WIDE]
        gram = gram - dot(left, above_gram, 0, 0)
        unit = unit - dot(left, above_unit, 0, 0)
    gram, unit = eliminate(gram, unit, first)
    upper[rows, :] = jnp.where(row_id + first <= col_id, gram, 0.0)
    inverse[rows, :] = unit


def factor_gram(gram_ref, upper, inverse):
    for first in range(0, K, WIDE):
        factor_rows(gram_ref, upper, inverse, first)


def prepare(staged, packed, base):
    def body(elem, carry):
        for pair in range(4):
            if pair < 3:
                right = staged[elem, 2 * pair + 1]
            else:
                right = jnp.zeros((DOF, DOF), F32)
            both = jnp.concatenate([staged[elem, 2 * pair], right], axis=1)
            for piece, value in enumerate(split(both)):
                packed[base + elem, piece, :, pair * 128 : (pair + 1) * 128] = value
        return carry

    lax.fori_loop(0, STAGED, body, 0, unroll=2)


def spread(source, elems, base, part):
    is_low = lax.broadcasted_iota(jnp.int32, (NARROW, 2 * DOF), 1) < DOF
    count = LAYER // 2 // PARTS

    def body(step, carry):
        pair = part * count + step
        straight = source[:, pl.ds(pl.multiple_of(pair * 128, 128), 128)]
        turned = pltpu.roll(straight, DOF, 1)
        for side, low, high in ((0, straight, turned), (1, turned, straight)):
            place = base + 2 * pair + side
            for piece, value in enumerate(split(jnp.where(is_low, low, 0.0))):
                elems[0, place, piece] = value
            for piece, value in enumerate(split(jnp.where(is_low, 0.0, high))):
                elems[1, place, piece] = value
        return carry

    lax.fori_loop(0, count, body, 0, unroll=8)


def solid(cavity, elem):
    return (1 - cavity[elem]).astype(F32)


def operate(faces, shift, cavity, elems, packed, out, own_rows, begin, end):
    def product(left, right):
        return lax.dot_general(
            left, right, (((1,), (1,)), ((), ())), preferred_element_type=F32
        )

    def one(elem):
        at = [LAYER + elem]
        for side in range(SIDES - 1):
            beside = faces[side, elem]
            at.append(jnp.where(beside < 0, NONE, jnp.clip(beside + shift, 0, NONE - 1)))
        pieces = []
        for piece in range(3):
            pairs = [
                elems[0, at[2 * pair], piece] + elems[1, at[2 * pair + 1], piece]
                for pair in range(3)
            ]
            pairs.append(elems[0, at[6], piece])
            pieces.append(jnp.concatenate(pairs, axis=1))
        three = product(jnp.concatenate(pieces, axis=0), packed[elem, 0])
        two = product(jnp.concatenate(pieces[:2], axis=0), packed[elem, 1])
        last = product(pieces[0], packed[elem, 2])
        small = three[2 * NARROW :] + two[NARROW:] + last
        value = three[:NARROW] + (three[NARROW : 2 * NARROW] + two[:NARROW] + small)
        return value * solid(cavity, elem)

    def body(pair, carry):
        cols = pl.ds(pl.multiple_of(pair * 128, 128), 128)
        out[own_rows, cols] = jnp.concatenate([one(2 * pair), one(2 * pair + 1)], axis=1)
        return carry

    lax.fori_loop(begin, end, body, 0, unroll=4)


def kernel(
    faces,
    cavity,
    start,
    blocks,
    basis_out,
    coef_out,
    basis,
    image,
    second,
    send_0,
    low_0,
    high_0,
    send_1,
    low_1,
    high_1,
    elems,
    packed,
    staged,
    near_0,
    far_0,
    done_0,
    near_1,
    far_1,
    done_1,
    near_2,
    far_2,
    done_2,
    near_3,
    far_3,
    done_3,
    part_0,
    part_1,
    part_2,
    part_3,
    gram,
    upper,
    inverse,
    alpha,
    flip,
    update,
    start_sem,
    stage_sem,
    halo_send,
    halo_recv,
    rows_send,
    rows_recv,
    sums_send,
    sums_recv,
):
    space = lax.axis_index("space")
    blk = lax.axis_index("blk")
    core = lax.rem(space, CORES)
    spot = lax.rem(space, XS * CORES)
    plane = space // (XS * CORES)
    plane_base = plane * (XS * CORES)
    quad = blk * CORES + core
    right = lax.rem(blk + 1, YS)
    left = lax.rem(blk + YS - 1, YS)
    shift = LAYER - space * LAYER
    own_rows = pl.ds(pl.multiple_of(blk * NARROW, NARROW), NARROW)
    right_rows = pl.ds(pl.multiple_of(right * NARROW, NARROW), NARROW)
    left_rows = pl.ds(pl.multiple_of(left * NARROW, NARROW), NARROW)
    above = (lax.rem(space + 1, SPACE), blk)
    below = (lax.rem(space + SPACE - 1, SPACE), blk)
    near_ids = [lax.rem(spot + step, 8) for step in range(1, 8)]
    near_devices = [(plane_base + near, blk) for near in near_ids]
    far_devices = [(lax.rem(plane + step, 8) * 8 + spot, blk) for step in range(1, 8)]
    quads = [lax.rem(quad + step, 8) for step in range(1, 8)]
    done_devices = [(space - core + lax.rem(q, CORES), q // CORES) for q in quads]

    def stage_copy(part):
        return pltpu.make_async_copy(
            blocks.at[pl.ds(part * STAGED, STAGED)], staged.at[part % 2], stage_sem.at[part % 2]
        )

    load_start = pltpu.make_async_copy(start, basis.at[own_rows], start_sem)
    load_start.start()
    stage_copy(0).start()
    stage_copy(1).start()
    barrier = pltpu.get_barrier_semaphore()
    for device in near_devices + far_devices + done_devices + [above, below]:
        pl.semaphore_signal(barrier, inc=1, device_id=device, device_id_type=MESH)

    def masked(array, rows, send, part):
        is_low = lax.broadcasted_iota(jnp.int32, (NARROW, 2 * DOF), 1) < DOF
        count = LAYER // 2 // PARTS
        for step in range(count):
            pair = part * count + step
            cols = pl.ds(pl.multiple_of(pair * 128, 128), 128)
            weight = jnp.where(is_low, solid(cavity, 2 * pair), solid(cavity, 2 * pair + 1))
            send[:, cols] = array[rows, cols] * weight

    def halo_copies(call, part, send, low, high):
        cols = pl.ds(pl.multiple_of(part * PART, PART), PART)
        return [
            pltpu.make_async_remote_copy(
                src_ref=send.at[:, cols],
                dst_ref=target.at[:, cols],
                send_sem=halo_send.at[call, way, part],
                recv_sem=halo_recv.at[call, way, part],
                device_id=device,
                device_id_type=MESH,
            )
            for way, target, device in ((0, low, above), (1, high, below))
        ]

    def rows_copy(call, slot, array, rows, half, target):
        place = array.at[rows, pl.ds(half * HALF, HALF)]
        return pltpu.make_async_remote_copy(
            src_ref=place,
            dst_ref=place,
            send_sem=rows_send.at[call, slot],
            recv_sem=rows_recv.at[call, slot],
            device_id=(space, target),
            device_id_type=MESH,
        )

    def gather(call, array, half):
        copies = [
            rows_copy(call, 2 * half, array, own_rows, half, (right, left)[half]),
            rows_copy(call, 2 * half + 1, array, own_rows, half, (left, right)[half]),
        ]
        for copy in copies:
            copy.start()
        return copies

    def relay(call, array, copies):
        copies[0].wait_recv()
        onward = rows_copy(call, 4, array, left_rows, 0, right)
        onward.start()
        copies[2].wait_recv()
        back = rows_copy(call, 5, array, right_rows, 1, left)
        back.start()
        return copies + [onward, back]

    def gathered(copies):
        for slot, copy in enumerate(copies):
            if slot not in (0, 2):
                copy.wait_recv()
        for copy in copies:
            copy.wait_send()

    sent = []

    def wait(copies):
        for copy in copies:
            copy.wait_recv()
        sent.extend(copies)

    def exchange(call, stage, sources, slots, mine, devices):
        copies = []
        for step in range(7):
            copy = pltpu.make_async_remote_copy(
                src_ref=sources[step],
                dst_ref=slots.at[mine],
                send_sem=sums_send.at[call, stage, step],
                recv_sem=sums_recv.at[call, stage, step],
                device_id=devices[step],
                device_id_type=MESH,
            )
            copy.start()
            copies.append(copy)
        return copies

    def total(slots):
        value = slots[0]
        for slot in range(1, 8):
            value = value + slots[slot]
        return value

    def reduce_near(call, part, near):
        half = part.shape[0] // CORES
        sources = [
            part.at[pl.ds(pl.multiple_of(lax.rem(spot_id, CORES) * half, 8), half)]
            for spot_id in near_ids
        ]
        copies = exchange(call, 0, sources, near, spot, near_devices)
        near[spot] = part[pl.ds(pl.multiple_of(core * half, 8), half), :]
        return copies

    def reduce_far(call, copies, near, far):
        wait(copies)
        far[plane] = total(near)
        return exchange(call, 1, [far.at[plane]] * 7, far, plane, far_devices)

    def reduce_done(call, copies, far, done):
        wait(copies)
        done[quad] = total(far)
        return exchange(call, 2, [done.at[quad]] * 7, done, quad, done_devices)

    def square(done, which):
        rows = []
        for member in range(YS):
            panel = jnp.concatenate([done[2 * member], done[2 * member + 1]], axis=0)
            rows.append(panel[which * NARROW : (which + 1) * NARROW])
        return jnp.concatenate(rows, axis=0)

    def over_chunks(body, init):
        def step(chunk, carry):
            return body(pl.ds(pl.multiple_of(chunk * CHUNK, CHUNK), CHUNK), carry)

        return lax.fori_loop(0, ROWS // CHUNK, step, init)

    def over_parts(body):
        def step(part, carry):
            body(part)
            return carry

        lax.fori_loop(0, PARTS, step, 0)

    def keep_upper(which):
        flip[...] = upper[...].T
        coef_out[which] = flip[own_rows, :]

    def receive(call, send, low, high, first, count):
        def body(step, carry):
            part = first + step
            for copy in halo_copies(call, part, send, low, high):
                copy.wait()
            spread(low, elems, 0, part)
            spread(high, elems, 2 * LAYER, part)
            return carry

        lax.fori_loop(0, count, body, 0)

    def apply(out, begin, end):
        operate(faces, shift, cavity, elems, packed, out, own_rows, begin, end)

    load_start.wait()
    over_parts(lambda part: masked(basis, own_rows, send_0, part))
    pl.semaphore_wait(barrier, 23)

    def start_halo(part):
        for copy in halo_copies(0, part, send_0, low_0, high_0):
            copy.start()

    over_parts(start_halo)
    start_copies = gather(0, basis, 0) + gather(0, basis, 1)
    for part in range(LAYER // STAGED):
        stage_copy(part).wait()
        prepare(staged.at[part % 2], packed, part * STAGED)
        if part + 2 < LAYER // STAGED:
            stage_copy(part + 2).start()
    for which in range(2):
        for piece in range(3):
            elems[which, NONE, piece] = jnp.zeros((NARROW, 2 * DOF), BF16)
    over_parts(lambda part: spread(send_0, elems, LAYER, part))
    start_copies = relay(0, basis, start_copies)
    receive(0, send_0, low_0, high_0, 0, PARTS)
    apply(image, 0, LAYER // 2)
    gathered(start_copies)
    image_copies = gather(1, image, 0) + gather(1, image, 1)

    def start_products(cols, carry):
        own = jnp.concatenate([basis[own_rows, cols], image[own_rows, cols]], axis=0)
        return carry + cross(own, basis[:, cols])

    part_0[...] = over_chunks(start_products, jnp.zeros(part_0.shape, F32))
    sums = reduce_near(0, part_0, near_0)
    sums = reduce_far(0, sums, near_0, far_0)
    sums = reduce_done(0, sums, far_0, done_0)
    image_copies = relay(1, image, image_copies)
    wait(sums)
    gram[...] = square(done_0, 0)
    factor_gram(gram, upper, inverse)
    alpha[...] = cross(times(inverse[...], square(done_0, 1)), inverse[...])
    update[:, pl.ds(0, K)] = inverse[...]
    update[:, pl.ds(K, K)] = -times(alpha[...], inverse[...])
    gathered(image_copies)

    def first_residue(part):
        for side in range(PART // CHUNK):
            cols = pl.ds(pl.multiple_of(part * PART + side * CHUNK, CHUNK), CHUNK)
            both = jnp.concatenate([image[:, cols], basis[:, cols]], axis=0)
            image[:, cols] = times(update[...], both)
        masked(image, own_rows, send_1, part)
        for copy in halo_copies(1, part, send_1, low_1, high_1):
            copy.start()

    over_parts(first_residue)

    def residue_products(cols, carry):
        own = image[own_rows, cols]
        vectors = times(inverse[...], basis[:, cols])
        basis[:, cols] = vectors
        return carry[0] + cross(own, image[:, cols]), carry[1] + cross(own, vectors)

    empty = jnp.zeros((NARROW, K), F32)
    products = over_chunks(residue_products, (empty, empty))
    part_1[pl.ds(0, NARROW), :] = products[0]
    part_1[pl.ds(NARROW, NARROW), :] = products[1]
    sums = reduce_near(1, part_1, near_1)
    coef_out[1] = alpha[own_rows, :]
    keep_upper(0)
    over_parts(lambda part: spread(send_1, elems, LAYER, part))
    receive(1, send_1, low_1, high_1, 0, 2)
    sums = reduce_far(1, sums, near_1, far_1)
    receive(1, send_1, low_1, high_1, 2, 2)
    apply(second, 0, LAYER // 4)
    sums = reduce_done(1, sums, far_1, done_1)
    second_copies = gather(2, second, 0)
    apply(second, LAYER // 4, LAYER // 2)
    second_copies += gather(2, second, 1)

    def image_products(cols, carry):
        return carry + cross(second[own_rows, cols], image[:, cols])

    part_2[...] = over_chunks(image_products, empty)
    inner_sums = reduce_near(2, part_2, near_2)
    wait(sums)
    gram[...] = square(done_1, 0)
    factor_gram(gram, upper, inverse)
    skew = cross(upper[...], times(inverse[...], square(done_1, 1)))
    inner_sums = reduce_far(2, inner_sums, near_2, far_2)
    second_copies = relay(2, second, second_copies)
    update[:, pl.ds(0, K)] = inverse[...]

    def second_basis(cols, carry):
        image[:, cols] = times(inverse[...], image[:, cols])
        basis[:, cols] = times(upper[...], basis[:, cols])
        return carry

    over_chunks(second_basis, 0)
    inner_sums = reduce_done(2, inner_sums, far_2, done_2)
    keep_upper(2)
    wait(inner_sums)
    inner = cross(times(inverse[...], square(done_2, 0)), inverse[...])
    alpha[...] = inner - skew
    update[:, pl.ds(K, K)] = -alpha[...]
    gathered(second_copies)

    def second_residue(cols, carry):
        both = jnp.concatenate([second[:, cols], image[:, cols]], axis=0)
        value = times(update[...], both) - basis[:, cols]
        second[:, cols] = value
        return carry + cross(second[own_rows, cols], value)

    part_3[...] = over_chunks(second_residue, empty)
    sums = reduce_near(3, part_3, near_3)
    coef_out[3] = alpha[own_rows, :]
    sums = reduce_far(3, sums, near_3, far_3)
    wait(reduce_done(3, sums, far_3, done_3))
    gram[...] = square(done_3, 0)
    factor_gram(gram, upper, inverse)
    keep_upper(4)

    def last_basis(cols, carry):
        basis_out[:, cols] = times(inverse[own_rows, :], second[:, cols])
        return carry

    over_chunks(last_basis, 0)
    for copy in sent:
        copy.wait_send()


def local(start, faces, cavity, blocks):
    smem = pl.BlockSpec(memory_space=pltpu.SMEM)
    vmem = pl.BlockSpec(memory_space=pltpu.VMEM)

    def slots(rows):
        return [pltpu.VMEM((8, rows // CORES, K), F32)] * 3

    basis, coefficients = pl.pallas_call(
        kernel,
        out_shape=(
            jax.ShapeDtypeStruct((NARROW, ROWS), F32),
            jax.ShapeDtypeStruct((5, NARROW, K), F32),
        ),
        in_specs=[
            smem,
            smem,
            pl.BlockSpec(memory_space=pl.ANY),
            pl.BlockSpec(memory_space=pl.ANY),
        ],
        out_specs=(vmem, vmem),
        scratch_shapes=[pltpu.VMEM((K, ROWS), F32)] * 3
        + [pltpu.VMEM((NARROW, ROWS), F32)] * 6
        + [
            pltpu.VMEM((2, NONE + 1, 3, NARROW, 2 * DOF), BF16),
            pltpu.VMEM((LAYER, 3, DOF, 8 * DOF), BF16),
            pltpu.VMEM((2, STAGED, SIDES, DOF, DOF), F32),
        ]
        + slots(2 * NARROW)
        + slots(2 * NARROW)
        + slots(NARROW)
        + slots(NARROW)
        + [pltpu.VMEM((count * NARROW, K), F32) for count in (2, 2, 1, 1)]
        + [pltpu.VMEM((K, K), F32)] * 5
        + [pltpu.VMEM((K, 2 * K), F32)]
        + [
            pltpu.SemaphoreType.DMA,
            pltpu.SemaphoreType.DMA((2,)),
            pltpu.SemaphoreType.DMA((2, 2, PARTS)),
            pltpu.SemaphoreType.DMA((2, 2, PARTS)),
            pltpu.SemaphoreType.DMA((3, 6)),
            pltpu.SemaphoreType.DMA((3, 6)),
            pltpu.SemaphoreType.DMA((4, 3, 7)),
            pltpu.SemaphoreType.DMA((4, 3, 7)),
        ],
        compiler_params=pltpu.CompilerParams(
            collective_id=1, has_side_effects=True, vmem_limit_bytes=60 * 2**20
        ),
    )(faces.T, cavity, start.T, blocks)
    return basis.T, jnp.swapaxes(coefficients, 1, 2)


def solution(mesh):
    in_specs = (P("space", "blk"), P("space", None), P("space"), P("space", None, None, None))
    out_specs = (P("space", "blk"), P(None, None, "blk"))
    return jax.shard_map(local, mesh=mesh, in_specs=in_specs, out_specs=out_specs, check_vma=False)
```

```python
import jax
import jax.numpy as jnp
from jax import lax
from jax.experimental import pallas as pl
from jax.experimental.pallas import tpu as pltpu
from jax.sharding import PartitionSpec as P

LAYER = 64
DOF = 64
ROWS = LAYER * DOF
K = 128
CORES = 2
XS = 4
ZS = 8
YS = 4
SPACE = ZS * XS * CORES
NARROW = K // YS
SIDES = 7
PARTS = 4
PART = ROWS // PARTS
HALF = ROWS // 2
NONE = 3 * LAYER
WIDE = 32
SUB = 16
CHUNK = 512
STAGED = 16
MESH = pl.DeviceIdType.MESH
F32 = jnp.float32
BF16 = jnp.bfloat16


def dot(left, right, left_dim, right_dim):
    return lax.dot_general(
        left,
        right,
        (((left_dim,), (right_dim,)), ((), ())),
        precision=lax.Precision.HIGHEST,
        preferred_element_type=F32,
    )


def times(left, right):
    return dot(left, right, 1, 0)


def cross(left, right):
    return dot(left, right, 1, 1)


def split(value):
    first = value.astype(BF16)
    rest = value - first.astype(F32)
    second = rest.astype(BF16)
    return first, second, (rest - second.astype(F32)).astype(BF16)


def eliminate(gram, unit, first):
    shape = gram.shape
    row_id = lax.broadcasted_iota(jnp.int32, shape, 0)
    for sub in range(0, WIDE, SUB):
        columns = [
            jnp.broadcast_to(gram[:, first + sub + j : first + sub + j + 1], shape)
            for j in range(SUB)
        ]
        for j in range(SUB):
            k = sub + j
            scale = lax.rsqrt(jnp.broadcast_to(columns[j][k : k + 1], shape))
            pivot_gram = jnp.broadcast_to(gram[k : k + 1], shape) * scale
            pivot_unit = jnp.broadcast_to(unit[k : k + 1], shape) * scale
            below = jnp.where(row_id > k, columns[j], 0.0) * scale
            for other in range(j + 1, SUB):
                near = jnp.broadcast_to(columns[j][sub + other : sub + other + 1], shape)
                columns[other] = columns[other] - below * (near * scale)
            gram = jnp.where(row_id == k, pivot_gram, gram - below * pivot_gram)
            unit = jnp.where(row_id == k, pivot_unit, unit - below * pivot_unit)
    return gram, unit


def factor_rows(gram_ref, upper, inverse, first):
    row_id = lax.broadcasted_iota(jnp.int32, (WIDE, K), 0)
    col_id = lax.broadcasted_iota(jnp.int32, (WIDE, K), 1)
    rows = pl.ds(first, WIDE)
    gram = gram_ref[rows, :]
    unit = jnp.where(row_id + first == col_id, 1.0, 0.0)
    if first:
        above_gram = upper[pl.ds(0, first), :]
        above_unit = inverse[pl.ds(0, first), :]
        left = above_gram[:, first : first + WIDE]
        gram = gram - dot(left, above_gram, 0, 0)
        unit = unit - dot(left, above_unit, 0, 0)
    gram, unit = eliminate(gram, unit, first)
    upper[rows, :] = jnp.where(row_id + first <= col_id, gram, 0.0)
    inverse[rows, :] = unit


def factor_gram(gram_ref, upper, inverse):
    for first in range(0, K, WIDE):
        factor_rows(gram_ref, upper, inverse, first)


def prepare(staged, packed, base):
    def body(elem, carry):
        for pair in range(4):
            if pair < 3:
                right = staged[elem, 2 * pair + 1]
            else:
                right = jnp.zeros((DOF, DOF), F32)
            both = jnp.concatenate([staged[elem, 2 * pair], right], axis=1)
            for piece, value in enumerate(split(both)):
                packed[base + elem, piece, :, pair * 128 : (pair + 1) * 128] = value
        return carry

    lax.fori_loop(0, STAGED, body, 0, unroll=2)


def spread(source, elems, base, part):
    is_low = lax.broadcasted_iota(jnp.int32, (NARROW, 2 * DOF), 1) < DOF
    count = LAYER // 2 // PARTS

    def body(step, carry):
        pair = part * count + step
        straight = source[:, pl.ds(pl.multiple_of(pair * 128, 128), 128)]
        turned = pltpu.roll(straight, DOF, 1)
        for side, low, high in ((0, straight, turned), (1, turned, straight)):
            place = base + 2 * pair + side
            for piece, value in enumerate(split(jnp.where(is_low, low, 0.0))):
                elems[0, place, piece] = value
            for piece, value in enumerate(split(jnp.where(is_low, 0.0, high))):
                elems[1, place, piece] = value
        return carry

    lax.fori_loop(0, count, body, 0, unroll=8)


def solid(cavity, elem):
    return (1 - cavity[elem]).astype(F32)


def operate(faces, shift, cavity, elems, packed, out, own_rows, begin, end):
    def product(left, right):
        return lax.dot_general(
            left, right, (((1,), (1,)), ((), ())), preferred_element_type=F32
        )

    def one(elem):
        at = [LAYER + elem]
        for side in range(SIDES - 1):
            beside = faces[side, elem]
            at.append(jnp.where(beside < 0, NONE, jnp.clip(beside + shift, 0, NONE - 1)))
        pieces = []
        for piece in range(3):
            pairs = [
                elems[0, at[2 * pair], piece] + elems[1, at[2 * pair + 1], piece]
                for pair in range(3)
            ]
            pairs.append(elems[0, at[6], piece])
            pieces.append(jnp.concatenate(pairs, axis=1))
        three = product(jnp.concatenate(pieces, axis=0), packed[elem, 0])
        two = product(jnp.concatenate(pieces[:2], axis=0), packed[elem, 1])
        last = product(pieces[0], packed[elem, 2])
        small = three[2 * NARROW :] + two[NARROW:] + last
        value = three[:NARROW] + (three[NARROW : 2 * NARROW] + two[:NARROW] + small)
        return value * solid(cavity, elem)

    def body(pair, carry):
        cols = pl.ds(pl.multiple_of(pair * 128, 128), 128)
        out[own_rows, cols] = jnp.concatenate([one(2 * pair), one(2 * pair + 1)], axis=1)
        return carry

    lax.fori_loop(begin, end, body, 0, unroll=4)


def kernel(
    faces,
    cavity,
    start,
    blocks,
    basis_out,
    coef_out,
    basis,
    image,
    second,
    send_0,
    low_0,
    high_0,
    send_1,
    low_1,
    high_1,
    elems,
    packed,
    staged,
    near_0,
    far_0,
    done_0,
    near_1,
    far_1,
    done_1,
    near_2,
    far_2,
    done_2,
    near_3,
    far_3,
    done_3,
    part_0,
    part_1,
    part_2,
    part_3,
    gram,
    upper,
    inverse,
    alpha,
    flip,
    update,
    start_sem,
    stage_sem,
    halo_send,
    halo_recv,
    rows_send,
    rows_recv,
    sums_send,
    sums_recv,
):
    space = lax.axis_index("space")
    blk = lax.axis_index("blk")
    core = lax.rem(space, CORES)
    spot = lax.rem(space, XS * CORES)
    plane = space // (XS * CORES)
    plane_base = plane * (XS * CORES)
    quad = blk * CORES + core
    right = lax.rem(blk + 1, YS)
    left = lax.rem(blk + YS - 1, YS)
    shift = LAYER - space * LAYER
    own_rows = pl.ds(pl.multiple_of(blk * NARROW, NARROW), NARROW)
    right_rows = pl.ds(pl.multiple_of(right * NARROW, NARROW), NARROW)
    left_rows = pl.ds(pl.multiple_of(left * NARROW, NARROW), NARROW)
    above = (lax.rem(space + 1, SPACE), blk)
    below = (lax.rem(space + SPACE - 1, SPACE), blk)
    near_ids = [lax.rem(spot + step, 8) for step in range(1, 8)]
    near_devices = [(plane_base + near, blk) for near in near_ids]
    far_devices = [(lax.rem(plane + step, 8) * 8 + spot, blk) for step in range(1, 8)]
    quads = [lax.rem(quad + step, 8) for step in range(1, 8)]
    done_devices = [(space - core + lax.rem(q, CORES), q // CORES) for q in quads]

    def stage_copy(part):
        return pltpu.make_async_copy(
            blocks.at[pl.ds(part * STAGED, STAGED)], staged.at[part % 2], stage_sem.at[part % 2]
        )

    load_start = pltpu.make_async_copy(start, basis.at[own_rows], start_sem)
    load_start.start()
    stage_copy(0).start()
    stage_copy(1).start()
    barrier = pltpu.get_barrier_semaphore()
    for device in near_devices + far_devices + done_devices + [above, below]:
        pl.semaphore_signal(barrier, inc=1, device_id=device, device_id_type=MESH)

    def masked(array, rows, send, part):
        is_low = lax.broadcasted_iota(jnp.int32, (NARROW, 2 * DOF), 1) < DOF
        count = LAYER // 2 // PARTS
        for step in range(count):
            pair = part * count + step
            cols = pl.ds(pl.multiple_of(pair * 128, 128), 128)
            weight = jnp.where(is_low, solid(cavity, 2 * pair), solid(cavity, 2 * pair + 1))
            send[:, cols] = array[rows, cols] * weight

    def halo_copies(call, part, send, low, high):
        cols = pl.ds(pl.multiple_of(part * PART, PART), PART)
        return [
            pltpu.make_async_remote_copy(
                src_ref=send.at[:, cols],
                dst_ref=target.at[:, cols],
                send_sem=halo_send.at[call, way, part],
                recv_sem=halo_recv.at[call, way, part],
                device_id=device,
                device_id_type=MESH,
            )
            for way, target, device in ((0, low, above), (1, high, below))
        ]

    def rows_copy(call, slot, array, rows, half, target, source=None):
        place = array.at[rows, pl.ds(half * HALF, HALF)]
        return pltpu.make_async_remote_copy(
            src_ref=place if source is None else source.at[:, pl.ds(half * HALF, HALF)],
            dst_ref=place,
            send_sem=rows_send.at[call, slot],
            recv_sem=rows_recv.at[call, slot],
            device_id=(space, target),
            device_id_type=MESH,
        )

    def gather(call, array, half, source=None):
        copies = [
            rows_copy(call, 2 * half, array, own_rows, half, (right, left)[half], source),
            rows_copy(call, 2 * half + 1, array, own_rows, half, (left, right)[half], source),
        ]
        for copy in copies:
            copy.start()
        return copies

    def relay(call, array, copies):
        copies[0].wait_recv()
        onward = rows_copy(call, 4, array, left_rows, 0, right)
        onward.start()
        copies[2].wait_recv()
        back = rows_copy(call, 5, array, right_rows, 1, left)
        back.start()
        return copies + [onward, back]

    def gathered(copies):
        for slot, copy in enumerate(copies):
            if slot not in (0, 2):
                copy.wait_recv()
        for copy in copies:
            copy.wait_send()

    sent = []

    def wait(copies):
        for copy in copies:
            copy.wait_recv()
        sent.extend(copies)

    def exchange(call, stage, sources, slots, mine, devices):
        copies = []
        for step in range(7):
            copy = pltpu.make_async_remote_copy(
                src_ref=sources[step],
                dst_ref=slots.at[mine],
                send_sem=sums_send.at[call, stage, step],
                recv_sem=sums_recv.at[call, stage, step],
                device_id=devices[step],
                device_id_type=MESH,
            )
            copy.start()
            copies.append(copy)
        return copies

    def total(slots):
        value = slots[0]
        for slot in range(1, 8):
            value = value + slots[slot]
        return value

    def reduce_near(call, part, near):
        half = part.shape[0] // CORES
        sources = [
            part.at[pl.ds(pl.multiple_of(lax.rem(spot_id, CORES) * half, 8), half)]
            for spot_id in near_ids
        ]
        copies = exchange(call, 0, sources, near, spot, near_devices)
        near[spot] = part[pl.ds(pl.multiple_of(core * half, 8), half), :]
        return copies

    def reduce_far(call, copies, near, far):
        wait(copies)
        far[plane] = total(near)
        return exchange(call, 1, [far.at[plane]] * 7, far, plane, far_devices)

    def reduce_done(call, copies, far, done):
        wait(copies)
        done[quad] = total(far)
        return exchange(call, 2, [done.at[quad]] * 7, done, quad, done_devices)

    def square(done, which):
        rows = []
        for member in range(YS):
            panel = jnp.concatenate([done[2 * member], done[2 * member + 1]], axis=0)
            rows.append(panel[which * NARROW : (which + 1) * NARROW])
        return jnp.concatenate(rows, axis=0)

    def over_chunks(body, init):
        def step(chunk, carry):
            return body(pl.ds(pl.multiple_of(chunk * CHUNK, CHUNK), CHUNK), carry)

        return lax.fori_loop(0, ROWS // CHUNK, step, init)

    def over_parts(body):
        def step(part, carry):
            body(part)
            return carry

        lax.fori_loop(0, PARTS, step, 0)

    def keep_upper(which):
        flip[...] = upper[...].T
        coef_out[which] = flip[own_rows, :]

    def receive(call, send, low, high, first, count):
        def body(step, carry):
            part = first + step
            for copy in halo_copies(call, part, send, low, high):
                copy.wait()
            spread(low, elems, 0, part)
            spread(high, elems, 2 * LAYER, part)
            return carry

        lax.fori_loop(0, count, body, 0)

    def apply(out, begin, end):
        operate(faces, shift, cavity, elems, packed, out, own_rows, begin, end)

    load_start.wait()
    over_parts(lambda part: masked(basis, own_rows, send_0, part))
    pl.semaphore_wait(barrier, 23)
    start_copies = gather(0, basis, 0, start) + gather(0, basis, 1, start)

    def start_halo(part):
        for copy in halo_copies(0, part, send_0, low_0, high_0):
            copy.start()

    over_parts(start_halo)
    for part in range(LAYER // STAGED):
        stage_copy(part).wait()
        prepare(staged.at[part % 2], packed, part * STAGED)
        if part + 2 < LAYER // STAGED:
            stage_copy(part + 2).start()
    for which in range(2):
        for piece in range(3):
            elems[which, NONE, piece] = jnp.zeros((NARROW, 2 * DOF), BF16)
    over_parts(lambda part: spread(send_0, elems, LAYER, part))
    start_copies = relay(0, basis, start_copies)
    receive(0, send_0, low_0, high_0, 0, PARTS)
    apply(image, 0, LAYER // 2)
    gathered(start_copies)
    image_copies = gather(1, image, 0) + gather(1, image, 1)

    def start_products(cols, carry):
        own = jnp.concatenate([basis[own_rows, cols], image[own_rows, cols]], axis=0)
        return carry + cross(own, basis[:, cols])

    part_0[...] = over_chunks(start_products, jnp.zeros(part_0.shape, F32))
    sums = reduce_near(0, part_0, near_0)
    sums = reduce_far(0, sums, near_0, far_0)
    sums = reduce_done(0, sums, far_0, done_0)
    image_copies = relay(1, image, image_copies)
    wait(sums)
    gram[...] = square(done_0, 0)
    factor_gram(gram, upper, inverse)
    alpha[...] = cross(times(inverse[...], square(done_0, 1)), inverse[...])
    update[:, pl.ds(0, K)] = inverse[...]
    update[:, pl.ds(K, K)] = -times(alpha[...], inverse[...])
    gathered(image_copies)

    def first_residue(part):
        for side in range(PART // CHUNK):
            cols = pl.ds(pl.multiple_of(part * PART + side * CHUNK, CHUNK), CHUNK)
            both = jnp.concatenate([image[:, cols], basis[:, cols]], axis=0)
            image[:, cols] = times(update[...], both)
        masked(image, own_rows, send_1, part)
        for copy in halo_copies(1, part, send_1, low_1, high_1):
            copy.start()

    over_parts(first_residue)

    def residue_products(cols, carry):
        own = image[own_rows, cols]
        vectors = times(inverse[...], basis[:, cols])
        basis[:, cols] = vectors
        return carry[0] + cross(own, image[:, cols]), carry[1] + cross(own, vectors)

    empty = jnp.zeros((NARROW, K), F32)
    products = over_chunks(residue_products, (empty, empty))
    part_1[pl.ds(0, NARROW), :] = products[0]
    part_1[pl.ds(NARROW, NARROW), :] = products[1]
    sums = reduce_near(1, part_1, near_1)
    over_parts(lambda part: spread(send_1, elems, LAYER, part))
    receive(1, send_1, low_1, high_1, 0, PARTS)
    sums = reduce_far(1, sums, near_1, far_1)
    apply(second, 0, LAYER // 4)
    second_copies = gather(2, second, 0)
    apply(second, LAYER // 4, LAYER // 2)
    sums = reduce_done(1, sums, far_1, done_1)
    second_copies += gather(2, second, 1)

    def image_products(cols, carry):
        return carry + cross(second[own_rows, cols], image[:, cols])

    part_2[...] = over_chunks(image_products, empty)
    inner_sums = reduce_near(2, part_2, near_2)
    coef_out[1] = alpha[own_rows, :]
    keep_upper(0)
    wait(sums)
    gram[...] = square(done_1, 0)
    inner_sums = reduce_far(2, inner_sums, near_2, far_2)
    second_copies = relay(2, second, second_copies)
    factor_gram(gram, upper, inverse)
    skew = cross(upper[...], times(inverse[...], square(done_1, 1)))
    inner_sums = reduce_done(2, inner_sums, far_2, done_2)
    update[:, pl.ds(0, K)] = inverse[...]

    def second_basis(cols, carry):
        image[:, cols] = times(inverse[...], image[:, cols])
        basis[:, cols] = times(upper[...], basis[:, cols])
        return carry

    over_chunks(second_basis, 0)
    keep_upper(2)
    wait(inner_sums)
    inner = cross(times(inverse[...], square(done_2, 0)), inverse[...])
    alpha[...] = inner - skew
    update[:, pl.ds(K, K)] = -alpha[...]
    gathered(second_copies)

    def second_residue(cols, carry):
        both = jnp.concatenate([second[:, cols], image[:, cols]], axis=0)
        value = times(update[...], both) - basis[:, cols]
        second[:, cols] = value
        return carry + cross(second[own_rows, cols], value)

    part_3[...] = over_chunks(second_residue, empty)
    sums = reduce_near(3, part_3, near_3)
    coef_out[3] = alpha[own_rows, :]
    sums = reduce_far(3, sums, near_3, far_3)
    wait(reduce_done(3, sums, far_3, done_3))
    gram[...] = square(done_3, 0)
    factor_gram(gram, upper, inverse)
    keep_upper(4)

    def last_basis(cols, carry):
        basis_out[:, cols] = times(inverse[own_rows, :], second[:, cols])
        return carry

    over_chunks(last_basis, 0)
    for copy in sent:
        copy.wait_send()


def local(start, faces, cavity, blocks):
    smem = pl.BlockSpec(memory_space=pltpu.SMEM)
    vmem = pl.BlockSpec(memory_space=pltpu.VMEM)

    def slots(rows):
        return [pltpu.VMEM((8, rows // CORES, K), F32)] * 3

    basis, coefficients = pl.pallas_call(
        kernel,
        out_shape=(
            jax.ShapeDtypeStruct((NARROW, ROWS), F32),
            jax.ShapeDtypeStruct((5, NARROW, K), F32),
        ),
        in_specs=[
            smem,
            smem,
            pl.BlockSpec(memory_space=pl.ANY),
            pl.BlockSpec(memory_space=pl.ANY),
        ],
        out_specs=(vmem, vmem),
        scratch_shapes=[pltpu.VMEM((K, ROWS), F32)] * 3
        + [pltpu.VMEM((NARROW, ROWS), F32)] * 6
        + [
            pltpu.VMEM((2, NONE + 1, 3, NARROW, 2 * DOF), BF16),
            pltpu.VMEM((LAYER, 3, DOF, 8 * DOF), BF16),
            pltpu.VMEM((2, STAGED, SIDES, DOF, DOF), F32),
        ]
        + slots(2 * NARROW)
        + slots(2 * NARROW)
        + slots(NARROW)
        + slots(NARROW)
        + [pltpu.VMEM((count * NARROW, K), F32) for count in (2, 2, 1, 1)]
        + [pltpu.VMEM((K, K), F32)] * 5
        + [pltpu.VMEM((K, 2 * K), F32)]
        + [
            pltpu.SemaphoreType.DMA,
            pltpu.SemaphoreType.DMA((2,)),
            pltpu.SemaphoreType.DMA((2, 2, PARTS)),
            pltpu.SemaphoreType.DMA((2, 2, PARTS)),
            pltpu.SemaphoreType.DMA((3, 6)),
            pltpu.SemaphoreType.DMA((3, 6)),
            pltpu.SemaphoreType.DMA((4, 3, 7)),
            pltpu.SemaphoreType.DMA((4, 3, 7)),
        ],
        compiler_params=pltpu.CompilerParams(
            collective_id=1, has_side_effects=True, vmem_limit_bytes=60 * 2**20
        ),
    )(faces.T, cavity, start.T, blocks)
    return basis.T, jnp.swapaxes(coefficients, 1, 2)


def solution(mesh):
    in_specs = (P("space", "blk"), P("space", None), P("space"), P("space", None, None, None))
    out_specs = (P("space", "blk"), P(None, None, "blk"))
    return jax.shard_map(local, mesh=mesh, in_specs=in_specs, out_specs=out_specs, check_vma=False)
```

```python
import jax
import jax.numpy as jnp
from jax import lax
from jax.experimental import pallas as pl
from jax.experimental.pallas import tpu as pltpu
from jax.sharding import PartitionSpec as P

LAYER = 64
DOF = 64
ROWS = LAYER * DOF
K = 128
CORES = 2
XS = 4
ZS = 8
YS = 4
SPACE = ZS * XS * CORES
NARROW = K // YS
SIDES = 7
PARTS = 4
PART = ROWS // PARTS
HALF = ROWS // 2
NONE = 3 * LAYER
STEPS = (4, 3, 5, 2, 6, 1, 7)
WIDE = 32
SUB = 16
CHUNK = 512
STAGED = 16
MESH = pl.DeviceIdType.MESH
F32 = jnp.float32
BF16 = jnp.bfloat16


def dot(left, right, left_dim, right_dim):
    return lax.dot_general(
        left,
        right,
        (((left_dim,), (right_dim,)), ((), ())),
        precision=lax.Precision.HIGHEST,
        preferred_element_type=F32,
    )


def times(left, right):
    return dot(left, right, 1, 0)


def cross(left, right):
    return dot(left, right, 1, 1)


def split(value):
    first = value.astype(BF16)
    rest = value - first.astype(F32)
    second = rest.astype(BF16)
    return first, second, (rest - second.astype(F32)).astype(BF16)


def eliminate(gram, unit, first):
    shape = gram.shape
    row_id = lax.broadcasted_iota(jnp.int32, shape, 0)
    for sub in range(0, WIDE, SUB):
        columns = [
            jnp.broadcast_to(gram[:, first + sub + j : first + sub + j + 1], shape)
            for j in range(SUB)
        ]
        for j in range(SUB):
            k = sub + j
            scale = lax.rsqrt(jnp.broadcast_to(columns[j][k : k + 1], shape))
            pivot_gram = jnp.broadcast_to(gram[k : k + 1], shape) * scale
            pivot_unit = jnp.broadcast_to(unit[k : k + 1], shape) * scale
            below = jnp.where(row_id > k, columns[j], 0.0) * scale
            for other in range(j + 1, SUB):
                near = jnp.broadcast_to(columns[j][sub + other : sub + other + 1], shape)
                columns[other] = columns[other] - below * (near * scale)
            gram = jnp.where(row_id == k, pivot_gram, gram - below * pivot_gram)
            unit = jnp.where(row_id == k, pivot_unit, unit - below * pivot_unit)
    return gram, unit


def factor_rows(gram_ref, upper, inverse, first):
    row_id = lax.broadcasted_iota(jnp.int32, (WIDE, K), 0)
    col_id = lax.broadcasted_iota(jnp.int32, (WIDE, K), 1)
    rows = pl.ds(first, WIDE)
    gram = gram_ref[rows, :]
    unit = jnp.where(row_id + first == col_id, 1.0, 0.0)
    if first:
        above_gram = upper[pl.ds(0, first), :]
        above_unit = inverse[pl.ds(0, first), :]
        left = above_gram[:, first : first + WIDE]
        gram = gram - dot(left, above_gram, 0, 0)
        unit = unit - dot(left, above_unit, 0, 0)
    gram, unit = eliminate(gram, unit, first)
    upper[rows, :] = jnp.where(row_id + first <= col_id, gram, 0.0)
    inverse[rows, :] = unit


def factor_gram(gram_ref, upper, inverse):
    for first in range(0, K, WIDE):
        factor_rows(gram_ref, upper, inverse, first)


def prepare(staged, packed, base):
    def body(elem, carry):
        for pair in range(4):
            if pair < 3:
                right = staged[elem, 2 * pair + 1]
            else:
                right = jnp.zeros((DOF, DOF), F32)
            both = jnp.concatenate([staged[elem, 2 * pair], right], axis=1)
            for piece, value in enumerate(split(both)):
                packed[base + elem, piece, :, pair * 128 : (pair + 1) * 128] = value
        return carry

    lax.fori_loop(0, STAGED, body, 0, unroll=2)


def spread(source, elems, base, part):
    is_low = lax.broadcasted_iota(jnp.int32, (NARROW, 2 * DOF), 1) < DOF
    count = LAYER // 2 // PARTS

    def body(step, carry):
        pair = part * count + step
        straight = source[:, pl.ds(pl.multiple_of(pair * 128, 128), 128)]
        turned = pltpu.roll(straight, DOF, 1)
        for side, low, high in ((0, straight, turned), (1, turned, straight)):
            place = base + 2 * pair + side
            for piece, value in enumerate(split(jnp.where(is_low, low, 0.0))):
                elems[0, place, piece] = value
            for piece, value in enumerate(split(jnp.where(is_low, 0.0, high))):
                elems[1, place, piece] = value
        return carry

    lax.fori_loop(0, count, body, 0, unroll=8)


def solid(cavity, elem):
    return (1 - cavity[elem]).astype(F32)


def operate(faces, shift, cavity, elems, packed, out, own_rows, begin, end):
    def product(left, right):
        return lax.dot_general(
            left, right, (((1,), (1,)), ((), ())), preferred_element_type=F32
        )

    def one(elem):
        at = [LAYER + elem]
        for side in range(SIDES - 1):
            beside = faces[side, elem]
            at.append(jnp.where(beside < 0, NONE, jnp.clip(beside + shift, 0, NONE - 1)))
        pieces = []
        for piece in range(3):
            pairs = [
                elems[0, at[2 * pair], piece] + elems[1, at[2 * pair + 1], piece]
                for pair in range(3)
            ]
            pairs.append(elems[0, at[6], piece])
            pieces.append(jnp.concatenate(pairs, axis=1))
        three = product(jnp.concatenate(pieces, axis=0), packed[elem, 0])
        two = product(jnp.concatenate(pieces[:2], axis=0), packed[elem, 1])
        last = product(pieces[0], packed[elem, 2])
        small = three[2 * NARROW :] + two[NARROW:] + last
        value = three[:NARROW] + (three[NARROW : 2 * NARROW] + two[:NARROW] + small)
        return value * solid(cavity, elem)

    def body(pair, carry):
        cols = pl.ds(pl.multiple_of(pair * 128, 128), 128)
        out[own_rows, cols] = jnp.concatenate([one(2 * pair), one(2 * pair + 1)], axis=1)
        return carry

    lax.fori_loop(begin, end, body, 0, unroll=4)


def kernel(
    faces,
    cavity,
    start,
    blocks,
    basis_out,
    coef_out,
    basis,
    image,
    second,
    send_0,
    low_0,
    high_0,
    send_1,
    low_1,
    high_1,
    elems,
    packed,
    staged,
    near_0,
    far_0,
    done_0,
    near_1,
    far_1,
    done_1,
    near_2,
    far_2,
    done_2,
    near_3,
    far_3,
    done_3,
    part_0,
    part_1,
    part_2,
    part_3,
    gram,
    upper,
    inverse,
    alpha,
    flip,
    update,
    start_sem,
    stage_sem,
    halo_send,
    halo_recv,
    rows_send,
    rows_recv,
    sums_send,
    sums_recv,
):
    space = lax.axis_index("space")
    blk = lax.axis_index("blk")
    core = lax.rem(space, CORES)
    spot = lax.rem(space, XS * CORES)
    plane = space // (XS * CORES)
    plane_base = plane * (XS * CORES)
    quad = blk * CORES + core
    right = lax.rem(blk + 1, YS)
    left = lax.rem(blk + YS - 1, YS)
    shift = LAYER - space * LAYER
    own_rows = pl.ds(pl.multiple_of(blk * NARROW, NARROW), NARROW)
    right_rows = pl.ds(pl.multiple_of(right * NARROW, NARROW), NARROW)
    left_rows = pl.ds(pl.multiple_of(left * NARROW, NARROW), NARROW)
    above = (lax.rem(space + 1, SPACE), blk)
    below = (lax.rem(space + SPACE - 1, SPACE), blk)
    near_ids = [lax.rem(spot + step, 8) for step in STEPS]
    near_devices = [(plane_base + near, blk) for near in near_ids]
    far_devices = [(lax.rem(plane + step, 8) * 8 + spot, blk) for step in STEPS]
    quads = [lax.rem(quad + step, 8) for step in STEPS]
    done_devices = [(space - core + lax.rem(q, CORES), q // CORES) for q in quads]

    def stage_copy(part):
        return pltpu.make_async_copy(
            blocks.at[pl.ds(part * STAGED, STAGED)], staged.at[part % 2], stage_sem.at[part % 2]
        )

    load_start = pltpu.make_async_copy(start, basis.at[own_rows], start_sem)
    load_start.start()
    stage_copy(0).start()
    stage_copy(1).start()
    barrier = pltpu.get_barrier_semaphore()
    for device in near_devices + far_devices + done_devices + [above, below]:
        pl.semaphore_signal(barrier, inc=1, device_id=device, device_id_type=MESH)

    def masked(array, rows, send, part):
        is_low = lax.broadcasted_iota(jnp.int32, (NARROW, 2 * DOF), 1) < DOF
        count = LAYER // 2 // PARTS
        for step in range(count):
            pair = part * count + step
            cols = pl.ds(pl.multiple_of(pair * 128, 128), 128)
            weight = jnp.where(is_low, solid(cavity, 2 * pair), solid(cavity, 2 * pair + 1))
            send[:, cols] = array[rows, cols] * weight

    def halo_copies(call, part, send, low, high):
        cols = pl.ds(pl.multiple_of(part * PART, PART), PART)
        return [
            pltpu.make_async_remote_copy(
                src_ref=send.at[:, cols],
                dst_ref=target.at[:, cols],
                send_sem=halo_send.at[call, way, part],
                recv_sem=halo_recv.at[call, way, part],
                device_id=device,
                device_id_type=MESH,
            )
            for way, target, device in ((0, low, above), (1, high, below))
        ]

    def rows_copy(call, slot, array, rows, half, target, source=None):
        place = array.at[rows, pl.ds(half * HALF, HALF)]
        return pltpu.make_async_remote_copy(
            src_ref=place if source is None else source.at[:, pl.ds(half * HALF, HALF)],
            dst_ref=place,
            send_sem=rows_send.at[call, slot],
            recv_sem=rows_recv.at[call, slot],
            device_id=(space, target),
            device_id_type=MESH,
        )

    def gather(call, array, half, source=None):
        copies = [
            rows_copy(call, 2 * half, array, own_rows, half, (right, left)[half], source),
            rows_copy(call, 2 * half + 1, array, own_rows, half, (left, right)[half], source),
        ]
        for copy in copies:
            copy.start()
        return copies

    def relay(call, array, copies):
        copies[0].wait_recv()
        onward = rows_copy(call, 4, array, left_rows, 0, right)
        onward.start()
        copies[2].wait_recv()
        back = rows_copy(call, 5, array, right_rows, 1, left)
        back.start()
        return copies + [onward, back]

    def gathered(copies):
        for slot, copy in enumerate(copies):
            if slot not in (0, 2):
                copy.wait_recv()
        for copy in copies:
            copy.wait_send()

    sent = []

    def wait(copies):
        for copy in copies:
            copy.wait_recv()
        sent.extend(copies)

    def exchange(call, stage, sources, slots, mine, devices):
        copies = []
        for step in range(7):
            copy = pltpu.make_async_remote_copy(
                src_ref=sources[step],
                dst_ref=slots.at[mine],
                send_sem=sums_send.at[call, stage, step],
                recv_sem=sums_recv.at[call, stage, step],
                device_id=devices[step],
                device_id_type=MESH,
            )
            copy.start()
            copies.append(copy)
        return copies

    def total(slots):
        value = slots[0]
        for slot in range(1, 8):
            value = value + slots[slot]
        return value

    def reduce_near(call, part, near):
        half = part.shape[0] // CORES
        sources = [
            part.at[pl.ds(pl.multiple_of(lax.rem(spot_id, CORES) * half, 8), half)]
            for spot_id in near_ids
        ]
        copies = exchange(call, 0, sources, near, spot, near_devices)
        near[spot] = part[pl.ds(pl.multiple_of(core * half, 8), half), :]
        return copies

    def reduce_far(call, copies, near, far):
        wait(copies)
        far[plane] = total(near)
        return exchange(call, 1, [far.at[plane]] * 7, far, plane, far_devices)

    def reduce_done(call, copies, far, done):
        wait(copies)
        done[quad] = total(far)
        return exchange(call, 2, [done.at[quad]] * 7, done, quad, done_devices)

    def square(done, which):
        rows = []
        for member in range(YS):
            panel = jnp.concatenate([done[2 * member], done[2 * member + 1]], axis=0)
            rows.append(panel[which * NARROW : (which + 1) * NARROW])
        return jnp.concatenate(rows, axis=0)

    def over_chunks(body, init):
        def step(chunk, carry):
            return body(pl.ds(pl.multiple_of(chunk * CHUNK, CHUNK), CHUNK), carry)

        return lax.fori_loop(0, ROWS // CHUNK, step, init)

    def over_parts(body):
        def step(part, carry):
            body(part)
            return carry

        lax.fori_loop(0, PARTS, step, 0)

    def keep_upper(which):
        flip[...] = upper[...].T
        coef_out[which] = flip[own_rows, :]

    def receive(call, send, low, high, first, count):
        def body(step, carry):
            part = first + step
            for copy in halo_copies(call, part, send, low, high):
                copy.wait()
            spread(low, elems, 0, part)
            spread(high, elems, 2 * LAYER, part)
            return carry

        lax.fori_loop(0, count, body, 0)

    def apply(out, begin, end):
        operate(faces, shift, cavity, elems, packed, out, own_rows, begin, end)

    load_start.wait()
    over_parts(lambda part: masked(basis, own_rows, send_0, part))
    pl.semaphore_wait(barrier, 23)
    start_copies = gather(0, basis, 0, start) + gather(0, basis, 1, start)

    def start_halo(part):
        for copy in halo_copies(0, part, send_0, low_0, high_0):
            copy.start()

    over_parts(start_halo)
    for part in range(LAYER // STAGED):
        stage_copy(part).wait()
        prepare(staged.at[part % 2], packed, part * STAGED)
        if part + 2 < LAYER // STAGED:
            stage_copy(part + 2).start()
    for which in range(2):
        for piece in range(3):
            elems[which, NONE, piece] = jnp.zeros((NARROW, 2 * DOF), BF16)
    over_parts(lambda part: spread(send_0, elems, LAYER, part))
    start_copies = relay(0, basis, start_copies)
    receive(0, send_0, low_0, high_0, 0, PARTS)
    apply(image, 0, LAYER // 2)
    gathered(start_copies)
    image_copies = gather(1, image, 0) + gather(1, image, 1)

    def start_products(cols, carry):
        own = jnp.concatenate([basis[own_rows, cols], image[own_rows, cols]], axis=0)
        return carry + cross(own, basis[:, cols])

    part_0[...] = over_chunks(start_products, jnp.zeros(part_0.shape, F32))
    sums = reduce_near(0, part_0, near_0)
    sums = reduce_far(0, sums, near_0, far_0)
    sums = reduce_done(0, sums, far_0, done_0)
    image_copies = relay(1, image, image_copies)
    wait(sums)
    gram[...] = square(done_0, 0)
    factor_gram(gram, upper, inverse)
    alpha[...] = cross(times(inverse[...], square(done_0, 1)), inverse[...])
    update[:, pl.ds(0, K)] = inverse[...]
    update[:, pl.ds(K, K)] = -times(alpha[...], inverse[...])
    gathered(image_copies)

    def first_residue(part):
        for side in range(PART // CHUNK):
            cols = pl.ds(pl.multiple_of(part * PART + side * CHUNK, CHUNK), CHUNK)
            both = jnp.concatenate([image[:, cols], basis[:, cols]], axis=0)
            image[:, cols] = times(update[...], both)
        masked(image, own_rows, send_1, part)
        for copy in halo_copies(1, part, send_1, low_1, high_1):
            copy.start()

    over_parts(first_residue)

    def residue_products(cols, carry):
        own = image[own_rows, cols]
        vectors = times(inverse[...], basis[:, cols])
        basis[:, cols] = vectors
        return carry[0] + cross(own, image[:, cols]), carry[1] + cross(own, vectors)

    empty = jnp.zeros((NARROW, K), F32)
    products = over_chunks(residue_products, (empty, empty))
    part_1[pl.ds(0, NARROW), :] = products[0]
    part_1[pl.ds(NARROW, NARROW), :] = products[1]
    sums = reduce_near(1, part_1, near_1)
    over_parts(lambda part: spread(send_1, elems, LAYER, part))
    receive(1, send_1, low_1, high_1, 0, PARTS)
    sums = reduce_far(1, sums, near_1, far_1)
    apply(second, 0, LAYER // 4)
    second_copies = gather(2, second, 0)
    apply(second, LAYER // 4, LAYER // 2)
    sums = reduce_done(1, sums, far_1, done_1)
    second_copies += gather(2, second, 1)

    def image_products(cols, carry):
        return carry + cross(second[own_rows, cols], image[:, cols])

    part_2[...] = over_chunks(image_products, empty)
    inner_sums = reduce_near(2, part_2, near_2)
    coef_out[1] = alpha[own_rows, :]
    keep_upper(0)
    wait(sums)
    gram[...] = square(done_1, 0)
    inner_sums = reduce_far(2, inner_sums, near_2, far_2)
    second_copies = relay(2, second, second_copies)
    factor_gram(gram, upper, inverse)
    skew = cross(upper[...], times(inverse[...], square(done_1, 1)))
    inner_sums = reduce_done(2, inner_sums, far_2, done_2)
    update[:, pl.ds(0, K)] = inverse[...]

    def second_basis(cols, carry):
        image[:, cols] = times(inverse[...], image[:, cols])
        basis[:, cols] = times(upper[...], basis[:, cols])
        return carry

    over_chunks(second_basis, 0)
    keep_upper(2)
    wait(inner_sums)
    inner = cross(times(inverse[...], square(done_2, 0)), inverse[...])
    alpha[...] = inner - skew
    update[:, pl.ds(K, K)] = -alpha[...]
    gathered(second_copies)

    def second_residue(cols, carry):
        both = jnp.concatenate([second[:, cols], image[:, cols]], axis=0)
        value = times(update[...], both) - basis[:, cols]
        second[:, cols] = value
        return carry + cross(second[own_rows, cols], value)

    part_3[...] = over_chunks(second_residue, empty)
    sums = reduce_near(3, part_3, near_3)
    coef_out[3] = alpha[own_rows, :]
    sums = reduce_far(3, sums, near_3, far_3)
    wait(reduce_done(3, sums, far_3, done_3))
    gram[...] = square(done_3, 0)
    factor_gram(gram, upper, inverse)
    keep_upper(4)

    def last_basis(cols, carry):
        basis_out[:, cols] = times(inverse[own_rows, :], second[:, cols])
        return carry

    over_chunks(last_basis, 0)
    for copy in sent:
        copy.wait_send()


def local(start, faces, cavity, blocks):
    smem = pl.BlockSpec(memory_space=pltpu.SMEM)
    vmem = pl.BlockSpec(memory_space=pltpu.VMEM)

    def slots(rows):
        return [pltpu.VMEM((8, rows // CORES, K), F32)] * 3

    basis, coefficients = pl.pallas_call(
        kernel,
        out_shape=(
            jax.ShapeDtypeStruct((NARROW, ROWS), F32),
            jax.ShapeDtypeStruct((5, NARROW, K), F32),
        ),
        in_specs=[
            smem,
            smem,
            pl.BlockSpec(memory_space=pl.ANY),
            pl.BlockSpec(memory_space=pl.ANY),
        ],
        out_specs=(vmem, vmem),
        scratch_shapes=[pltpu.VMEM((K, ROWS), F32)] * 3
        + [pltpu.VMEM((NARROW, ROWS), F32)] * 6
        + [
            pltpu.VMEM((2, NONE + 1, 3, NARROW, 2 * DOF), BF16),
            pltpu.VMEM((LAYER, 3, DOF, 8 * DOF), BF16),
            pltpu.VMEM((2, STAGED, SIDES, DOF, DOF), F32),
        ]
        + slots(2 * NARROW)
        + slots(2 * NARROW)
        + slots(NARROW)
        + slots(NARROW)
        + [pltpu.VMEM((count * NARROW, K), F32) for count in (2, 2, 1, 1)]
        + [pltpu.VMEM((K, K), F32)] * 5
        + [pltpu.VMEM((K, 2 * K), F32)]
        + [
            pltpu.SemaphoreType.DMA,
            pltpu.SemaphoreType.DMA((2,)),
            pltpu.SemaphoreType.DMA((2, 2, PARTS)),
            pltpu.SemaphoreType.DMA((2, 2, PARTS)),
            pltpu.SemaphoreType.DMA((3, 6)),
            pltpu.SemaphoreType.DMA((3, 6)),
            pltpu.SemaphoreType.DMA((4, 3, 7)),
            pltpu.SemaphoreType.DMA((4, 3, 7)),
        ],
        compiler_params=pltpu.CompilerParams(
            collective_id=1, has_side_effects=True, vmem_limit_bytes=60 * 2**20
        ),
    )(faces.T, cavity, start.T, blocks)
    return basis.T, jnp.swapaxes(coefficients, 1, 2)


def solution(mesh):
    in_specs = (P("space", "blk"), P("space", None), P("space"), P("space", None, None, None))
    out_specs = (P("space", "blk"), P(None, None, "blk"))
    return jax.shard_map(local, mesh=mesh, in_specs=in_specs, out_specs=out_specs, check_vma=False)
```

```python
import jax
import jax.numpy as jnp
from jax import lax
from jax.experimental import pallas as pl
from jax.experimental.pallas import tpu as pltpu
from jax.sharding import PartitionSpec as P

LAYER = 64
DOF = 64
ROWS = LAYER * DOF
K = 128
CORES = 2
XS = 4
ZS = 8
YS = 4
SPACE = ZS * XS * CORES
NARROW = K // YS
SIDES = 7
PARTS = 4
PART = ROWS // PARTS
HALF = ROWS // 2
NONE = 3 * LAYER
STEPS = (4, 3, 5, 2, 6, 1, 7)
WIDE = 32
SUB = 16
CHUNK = 512
STAGED = 16
MESH = pl.DeviceIdType.MESH
F32 = jnp.float32
BF16 = jnp.bfloat16


def dot(left, right, left_dim, right_dim):
    return lax.dot_general(
        left,
        right,
        (((left_dim,), (right_dim,)), ((), ())),
        precision=lax.Precision.HIGHEST,
        preferred_element_type=F32,
    )


def times(left, right):
    return dot(left, right, 1, 0)


def cross(left, right):
    return dot(left, right, 1, 1)


def split(value):
    first = value.astype(BF16)
    rest = value - first.astype(F32)
    second = rest.astype(BF16)
    return first, second, (rest - second.astype(F32)).astype(BF16)


def eliminate(gram, unit, first):
    shape = gram.shape
    row_id = lax.broadcasted_iota(jnp.int32, shape, 0)
    for sub in range(0, WIDE, SUB):
        columns = [
            jnp.broadcast_to(gram[:, first + sub + j : first + sub + j + 1], shape)
            for j in range(SUB)
        ]
        for j in range(SUB):
            k = sub + j
            scale = lax.rsqrt(jnp.broadcast_to(columns[j][k : k + 1], shape))
            pivot_gram = jnp.broadcast_to(gram[k : k + 1], shape) * scale
            pivot_unit = jnp.broadcast_to(unit[k : k + 1], shape) * scale
            below = jnp.where(row_id > k, columns[j], 0.0) * scale
            for other in range(j + 1, SUB):
                near = jnp.broadcast_to(columns[j][sub + other : sub + other + 1], shape)
                columns[other] = columns[other] - below * (near * scale)
            gram = jnp.where(row_id == k, pivot_gram, gram - below * pivot_gram)
            unit = jnp.where(row_id == k, pivot_unit, unit - below * pivot_unit)
    return gram, unit


def factor_rows(gram_ref, upper, inverse, first):
    row_id = lax.broadcasted_iota(jnp.int32, (WIDE, K), 0)
    col_id = lax.broadcasted_iota(jnp.int32, (WIDE, K), 1)
    rows = pl.ds(first, WIDE)
    gram = gram_ref[rows, :]
    unit = jnp.where(row_id + first == col_id, 1.0, 0.0)
    if first:
        above_gram = upper[pl.ds(0, first), :]
        above_unit = inverse[pl.ds(0, first), :]
        left = above_gram[:, first : first + WIDE]
        gram = gram - dot(left, above_gram, 0, 0)
        unit = unit - dot(left, above_unit, 0, 0)
    gram, unit = eliminate(gram, unit, first)
    upper[rows, :] = jnp.where(row_id + first <= col_id, gram, 0.0)
    inverse[rows, :] = unit


def factor_gram(gram_ref, upper, inverse):
    for first in range(0, K, WIDE):
        factor_rows(gram_ref, upper, inverse, first)


def prepare(staged, packed, base):
    def body(elem, carry):
        for pair in range(4):
            if pair < 3:
                right = staged[elem, 2 * pair + 1]
            else:
                right = jnp.zeros((DOF, DOF), F32)
            both = jnp.concatenate([staged[elem, 2 * pair], right], axis=1)
            for piece, value in enumerate(split(both)):
                packed[base + elem, piece, :, pair * 128 : (pair + 1) * 128] = value
        return carry

    lax.fori_loop(0, STAGED, body, 0, unroll=2)


def spread(source, elems, base, part):
    is_low = lax.broadcasted_iota(jnp.int32, (NARROW, 2 * DOF), 1) < DOF
    count = LAYER // 2 // PARTS

    def body(step, carry):
        pair = part * count + step
        straight = source[:, pl.ds(pl.multiple_of(pair * 128, 128), 128)]
        turned = pltpu.roll(straight, DOF, 1)
        for side, low, high in ((0, straight, turned), (1, turned, straight)):
            place = base + 2 * pair + side
            for piece, value in enumerate(split(jnp.where(is_low, low, 0.0))):
                elems[0, place, piece] = value
            for piece, value in enumerate(split(jnp.where(is_low, 0.0, high))):
                elems[1, place, piece] = value
        return carry

    lax.fori_loop(0, count, body, 0, unroll=8)


def solid(cavity, elem):
    return (1 - cavity[elem]).astype(F32)


def operate(faces, shift, cavity, elems, packed, out, own_rows, begin, end):
    def product(left, right):
        return lax.dot_general(
            left, right, (((1,), (1,)), ((), ())), preferred_element_type=F32
        )

    def one(elem):
        at = [LAYER + elem]
        for side in range(SIDES - 1):
            beside = faces[side, elem]
            at.append(jnp.where(beside < 0, NONE, jnp.clip(beside + shift, 0, NONE - 1)))
        pieces = []
        for piece in range(3):
            pairs = [
                elems[0, at[2 * pair], piece] + elems[1, at[2 * pair + 1], piece]
                for pair in range(3)
            ]
            pairs.append(elems[0, at[6], piece])
            pieces.append(jnp.concatenate(pairs, axis=1))
        three = product(jnp.concatenate(pieces, axis=0), packed[elem, 0])
        two = product(jnp.concatenate(pieces[:2], axis=0), packed[elem, 1])
        last = product(pieces[0], packed[elem, 2])
        small = three[2 * NARROW :] + two[NARROW:] + last
        value = three[:NARROW] + (three[NARROW : 2 * NARROW] + two[:NARROW] + small)
        return value * solid(cavity, elem)

    def body(pair, carry):
        cols = pl.ds(pl.multiple_of(pair * 128, 128), 128)
        out[own_rows, cols] = jnp.concatenate([one(2 * pair), one(2 * pair + 1)], axis=1)
        return carry

    lax.fori_loop(begin, end, body, 0, unroll=4)


def kernel(
    faces,
    cavity,
    start,
    blocks,
    residue_out,
    gram_out,
    coef_out,
    basis,
    image,
    second,
    send_0,
    low_0,
    high_0,
    send_1,
    low_1,
    high_1,
    elems,
    packed,
    staged,
    near_0,
    far_0,
    done_0,
    near_1,
    far_1,
    done_1,
    near_2,
    far_2,
    done_2,
    near_3,
    far_3,
    done_3,
    part_0,
    part_1,
    part_2,
    part_3,
    gram,
    upper,
    inverse,
    alpha,
    flip,
    update,
    residue_sem,
    start_sem,
    stage_sem,
    halo_send,
    halo_recv,
    rows_send,
    rows_recv,
    sums_send,
    sums_recv,
):
    space = lax.axis_index("space")
    blk = lax.axis_index("blk")
    core = lax.rem(space, CORES)
    spot = lax.rem(space, XS * CORES)
    plane = space // (XS * CORES)
    plane_base = plane * (XS * CORES)
    quad = blk * CORES + core
    right = lax.rem(blk + 1, YS)
    left = lax.rem(blk + YS - 1, YS)
    shift = LAYER - space * LAYER
    own_rows = pl.ds(pl.multiple_of(blk * NARROW, NARROW), NARROW)
    right_rows = pl.ds(pl.multiple_of(right * NARROW, NARROW), NARROW)
    left_rows = pl.ds(pl.multiple_of(left * NARROW, NARROW), NARROW)
    above = (lax.rem(space + 1, SPACE), blk)
    below = (lax.rem(space + SPACE - 1, SPACE), blk)
    near_ids = [lax.rem(spot + step, 8) for step in STEPS]
    near_devices = [(plane_base + near, blk) for near in near_ids]
    far_devices = [(lax.rem(plane + step, 8) * 8 + spot, blk) for step in STEPS]
    quads = [lax.rem(quad + step, 8) for step in STEPS]
    done_devices = [(space - core + lax.rem(q, CORES), q // CORES) for q in quads]

    def stage_copy(part):
        return pltpu.make_async_copy(
            blocks.at[pl.ds(part * STAGED, STAGED)], staged.at[part % 2], stage_sem.at[part % 2]
        )

    load_start = pltpu.make_async_copy(start, basis.at[own_rows], start_sem)
    load_start.start()
    stage_copy(0).start()
    stage_copy(1).start()
    barrier = pltpu.get_barrier_semaphore()
    for device in near_devices + far_devices + done_devices + [above, below]:
        pl.semaphore_signal(barrier, inc=1, device_id=device, device_id_type=MESH)

    def masked(array, rows, send, part):
        is_low = lax.broadcasted_iota(jnp.int32, (NARROW, 2 * DOF), 1) < DOF
        count = LAYER // 2 // PARTS
        for step in range(count):
            pair = part * count + step
            cols = pl.ds(pl.multiple_of(pair * 128, 128), 128)
            weight = jnp.where(is_low, solid(cavity, 2 * pair), solid(cavity, 2 * pair + 1))
            send[:, cols] = array[rows, cols] * weight

    def halo_copies(call, part, send, low, high):
        cols = pl.ds(pl.multiple_of(part * PART, PART), PART)
        return [
            pltpu.make_async_remote_copy(
                src_ref=send.at[:, cols],
                dst_ref=target.at[:, cols],
                send_sem=halo_send.at[call, way, part],
                recv_sem=halo_recv.at[call, way, part],
                device_id=device,
                device_id_type=MESH,
            )
            for way, target, device in ((0, low, above), (1, high, below))
        ]

    def rows_copy(call, slot, array, rows, half, target, source=None):
        place = array.at[rows, pl.ds(half * HALF, HALF)]
        return pltpu.make_async_remote_copy(
            src_ref=place if source is None else source.at[:, pl.ds(half * HALF, HALF)],
            dst_ref=place,
            send_sem=rows_send.at[call, slot],
            recv_sem=rows_recv.at[call, slot],
            device_id=(space, target),
            device_id_type=MESH,
        )

    def gather(call, array, half, source=None):
        copies = [
            rows_copy(call, 2 * half, array, own_rows, half, (right, left)[half], source),
            rows_copy(call, 2 * half + 1, array, own_rows, half, (left, right)[half], source),
        ]
        for copy in copies:
            copy.start()
        return copies

    def relay(call, array, copies):
        copies[0].wait_recv()
        onward = rows_copy(call, 4, array, left_rows, 0, right)
        onward.start()
        copies[2].wait_recv()
        back = rows_copy(call, 5, array, right_rows, 1, left)
        back.start()
        return copies + [onward, back]

    def gathered(copies):
        for slot, copy in enumerate(copies):
            if slot not in (0, 2):
                copy.wait_recv()
        for copy in copies:
            copy.wait_send()

    sent = []

    def wait(copies):
        for copy in copies:
            copy.wait_recv()
        sent.extend(copies)

    def exchange(call, stage, sources, slots, mine, devices):
        copies = []
        for step in range(7):
            copy = pltpu.make_async_remote_copy(
                src_ref=sources[step],
                dst_ref=slots.at[mine],
                send_sem=sums_send.at[call, stage, step],
                recv_sem=sums_recv.at[call, stage, step],
                device_id=devices[step],
                device_id_type=MESH,
            )
            copy.start()
            copies.append(copy)
        return copies

    def total(slots):
        value = slots[0]
        for slot in range(1, 8):
            value = value + slots[slot]
        return value

    def reduce_near(call, part, near):
        half = part.shape[0] // CORES
        sources = [
            part.at[pl.ds(pl.multiple_of(lax.rem(spot_id, CORES) * half, 8), half)]
            for spot_id in near_ids
        ]
        copies = exchange(call, 0, sources, near, spot, near_devices)
        near[spot] = part[pl.ds(pl.multiple_of(core * half, 8), half), :]
        return copies

    def reduce_far(call, copies, near, far):
        wait(copies)
        far[plane] = total(near)
        return exchange(call, 1, [far.at[plane]] * 7, far, plane, far_devices)

    def reduce_done(call, copies, far, done):
        wait(copies)
        done[quad] = total(far)
        return exchange(call, 2, [done.at[quad]] * 7, done, quad, done_devices)

    def square(done, which):
        rows = []
        for member in range(YS):
            panel = jnp.concatenate([done[2 * member], done[2 * member + 1]], axis=0)
            rows.append(panel[which * NARROW : (which + 1) * NARROW])
        return jnp.concatenate(rows, axis=0)

    def over_chunks(body, init):
        def step(chunk, carry):
            return body(pl.ds(pl.multiple_of(chunk * CHUNK, CHUNK), CHUNK), carry)

        return lax.fori_loop(0, ROWS // CHUNK, step, init)

    def over_parts(body):
        def step(part, carry):
            body(part)
            return carry

        lax.fori_loop(0, PARTS, step, 0)

    def keep_upper(which):
        flip[...] = upper[...].T
        coef_out[which] = flip[own_rows, :]

    def receive(call, send, low, high, first, count):
        def body(step, carry):
            part = first + step
            for copy in halo_copies(call, part, send, low, high):
                copy.wait()
            spread(low, elems, 0, part)
            spread(high, elems, 2 * LAYER, part)
            return carry

        lax.fori_loop(0, count, body, 0)

    def apply(out, begin, end):
        operate(faces, shift, cavity, elems, packed, out, own_rows, begin, end)

    load_start.wait()
    over_parts(lambda part: masked(basis, own_rows, send_0, part))
    pl.semaphore_wait(barrier, 23)
    start_copies = gather(0, basis, 0, start) + gather(0, basis, 1, start)

    def start_halo(part):
        for copy in halo_copies(0, part, send_0, low_0, high_0):
            copy.start()

    over_parts(start_halo)
    for part in range(LAYER // STAGED):
        stage_copy(part).wait()
        prepare(staged.at[part % 2], packed, part * STAGED)
        if part + 2 < LAYER // STAGED:
            stage_copy(part + 2).start()
    for which in range(2):
        for piece in range(3):
            elems[which, NONE, piece] = jnp.zeros((NARROW, 2 * DOF), BF16)
    over_parts(lambda part: spread(send_0, elems, LAYER, part))
    start_copies = relay(0, basis, start_copies)
    receive(0, send_0, low_0, high_0, 0, PARTS)
    apply(image, 0, LAYER // 2)
    gathered(start_copies)
    image_copies = gather(1, image, 0) + gather(1, image, 1)

    def start_products(cols, carry):
        own = jnp.concatenate([basis[own_rows, cols], image[own_rows, cols]], axis=0)
        return carry + cross(own, basis[:, cols])

    part_0[...] = over_chunks(start_products, jnp.zeros(part_0.shape, F32))
    sums = reduce_near(0, part_0, near_0)
    sums = reduce_far(0, sums, near_0, far_0)
    sums = reduce_done(0, sums, far_0, done_0)
    image_copies = relay(1, image, image_copies)
    wait(sums)
    gram[...] = square(done_0, 0)
    factor_gram(gram, upper, inverse)
    alpha[...] = cross(times(inverse[...], square(done_0, 1)), inverse[...])
    update[:, pl.ds(0, K)] = inverse[...]
    update[:, pl.ds(K, K)] = -times(alpha[...], inverse[...])
    gathered(image_copies)

    def first_residue(part):
        for side in range(PART // CHUNK):
            cols = pl.ds(pl.multiple_of(part * PART + side * CHUNK, CHUNK), CHUNK)
            both = jnp.concatenate([image[:, cols], basis[:, cols]], axis=0)
            image[:, cols] = times(update[...], both)
        masked(image, own_rows, send_1, part)
        for copy in halo_copies(1, part, send_1, low_1, high_1):
            copy.start()

    over_parts(first_residue)

    def residue_products(cols, carry):
        own = image[own_rows, cols]
        vectors = times(inverse[...], basis[:, cols])
        basis[:, cols] = vectors
        return carry[0] + cross(own, image[:, cols]), carry[1] + cross(own, vectors)

    empty = jnp.zeros((NARROW, K), F32)
    products = over_chunks(residue_products, (empty, empty))
    part_1[pl.ds(0, NARROW), :] = products[0]
    part_1[pl.ds(NARROW, NARROW), :] = products[1]
    sums = reduce_near(1, part_1, near_1)
    over_parts(lambda part: spread(send_1, elems, LAYER, part))
    receive(1, send_1, low_1, high_1, 0, PARTS)
    sums = reduce_far(1, sums, near_1, far_1)
    apply(second, 0, LAYER // 4)
    second_copies = gather(2, second, 0)
    apply(second, LAYER // 4, LAYER // 2)
    sums = reduce_done(1, sums, far_1, done_1)
    second_copies += gather(2, second, 1)

    def image_products(cols, carry):
        return carry + cross(second[own_rows, cols], image[:, cols])

    part_2[...] = over_chunks(image_products, empty)
    inner_sums = reduce_near(2, part_2, near_2)
    coef_out[1] = alpha[own_rows, :]
    keep_upper(0)
    wait(sums)
    gram[...] = square(done_1, 0)
    inner_sums = reduce_far(2, inner_sums, near_2, far_2)
    second_copies = relay(2, second, second_copies)
    factor_gram(gram, upper, inverse)
    skew = cross(upper[...], times(inverse[...], square(done_1, 1)))
    inner_sums = reduce_done(2, inner_sums, far_2, done_2)
    update[:, pl.ds(0, K)] = inverse[...]

    def second_basis(cols, carry):
        image[:, cols] = times(inverse[...], image[:, cols])
        basis[:, cols] = times(upper[...], basis[:, cols])
        return carry

    over_chunks(second_basis, 0)
    keep_upper(2)
    wait(inner_sums)
    inner = cross(times(inverse[...], square(done_2, 0)), inverse[...])
    alpha[...] = inner - skew
    update[:, pl.ds(K, K)] = -alpha[...]
    gathered(second_copies)

    def second_residue(cols, carry):
        both = jnp.concatenate([second[:, cols], image[:, cols]], axis=0)
        value = times(update[...], both) - basis[:, cols]
        second[:, cols] = value
        return carry + cross(second[own_rows, cols], value)

    part_3[...] = over_chunks(second_residue, empty)
    sums = reduce_near(3, part_3, near_3)
    store_residue = pltpu.make_async_copy(second, residue_out, residue_sem)
    store_residue.start()
    coef_out[3] = alpha[own_rows, :]
    sums = reduce_far(3, sums, near_3, far_3)
    wait(reduce_done(3, sums, far_3, done_3))
    gram_out[...] = square(done_3, 0)
    store_residue.wait()
    for copy in sent:
        copy.wait_send()


def finish_kernel(residue, gram, coef, basis_out, coef_out, vectors, upper, inverse, flip, sem):
    own_rows = pl.ds(pl.multiple_of(lax.axis_index("blk") * NARROW, NARROW), NARROW)
    load = pltpu.make_async_copy(residue, vectors, sem)
    load.start()
    coef_out[pl.ds(0, 4)] = coef[...]
    factor_gram(gram, upper, inverse)
    flip[...] = upper[...].T
    coef_out[4] = flip[own_rows, :]
    load.wait()

    def last_basis(chunk, carry):
        cols = pl.ds(pl.multiple_of(chunk * CHUNK, CHUNK), CHUNK)
        basis_out[:, cols] = times(inverse[own_rows, :], vectors[:, cols])
        return carry

    lax.fori_loop(0, ROWS // CHUNK, last_basis, 0)


def local(start, faces, cavity, blocks):
    smem = pl.BlockSpec(memory_space=pltpu.SMEM)
    vmem = pl.BlockSpec(memory_space=pltpu.VMEM)

    def slots(rows):
        return [pltpu.VMEM((8, rows // CORES, K), F32)] * 3

    residue, gram, coefficients = pl.pallas_call(
        kernel,
        out_shape=(
            jax.ShapeDtypeStruct((K, ROWS), F32),
            jax.ShapeDtypeStruct((K, K), F32),
            jax.ShapeDtypeStruct((4, NARROW, K), F32),
        ),
        in_specs=[
            smem,
            smem,
            pl.BlockSpec(memory_space=pl.ANY),
            pl.BlockSpec(memory_space=pl.ANY),
        ],
        out_specs=(pl.BlockSpec(memory_space=pl.ANY), vmem, vmem),
        scratch_shapes=[pltpu.VMEM((K, ROWS), F32)] * 3
        + [pltpu.VMEM((NARROW, ROWS), F32)] * 6
        + [
            pltpu.VMEM((2, NONE + 1, 3, NARROW, 2 * DOF), BF16),
            pltpu.VMEM((LAYER, 3, DOF, 8 * DOF), BF16),
            pltpu.VMEM((2, STAGED, SIDES, DOF, DOF), F32),
        ]
        + slots(2 * NARROW)
        + slots(2 * NARROW)
        + slots(NARROW)
        + slots(NARROW)
        + [pltpu.VMEM((count * NARROW, K), F32) for count in (2, 2, 1, 1)]
        + [pltpu.VMEM((K, K), F32)] * 5
        + [pltpu.VMEM((K, 2 * K), F32)]
        + [
            pltpu.SemaphoreType.DMA,
            pltpu.SemaphoreType.DMA,
            pltpu.SemaphoreType.DMA((2,)),
            pltpu.SemaphoreType.DMA((2, 2, PARTS)),
            pltpu.SemaphoreType.DMA((2, 2, PARTS)),
            pltpu.SemaphoreType.DMA((3, 6)),
            pltpu.SemaphoreType.DMA((3, 6)),
            pltpu.SemaphoreType.DMA((4, 3, 7)),
            pltpu.SemaphoreType.DMA((4, 3, 7)),
        ],
        compiler_params=pltpu.CompilerParams(
            collective_id=1, has_side_effects=True, vmem_limit_bytes=60 * 2**20
        ),
    )(faces.T, cavity, start.T, blocks)
    basis, coefficients = pl.pallas_call(
        finish_kernel,
        out_shape=(
            jax.ShapeDtypeStruct((NARROW, ROWS), F32),
            jax.ShapeDtypeStruct((5, NARROW, K), F32),
        ),
        in_specs=[pl.BlockSpec(memory_space=pl.ANY), vmem, vmem],
        out_specs=(vmem, vmem),
        scratch_shapes=[pltpu.VMEM((K, ROWS), F32)]
        + [pltpu.VMEM((K, K), F32)] * 3
        + [pltpu.SemaphoreType.DMA],
        compiler_params=pltpu.CompilerParams(vmem_limit_bytes=63 * 2**20),
    )(residue, gram, coefficients)
    return basis.T, jnp.swapaxes(coefficients, 1, 2)


def solution(mesh):
    in_specs = (P("space", "blk"), P("space", None), P("space"), P("space", None, None, None))
    out_specs = (P("space", "blk"), P(None, None, "blk"))
    return jax.shard_map(local, mesh=mesh, in_specs=in_specs, out_specs=out_specs, check_vma=False)
```

```python
import jax
import jax.numpy as jnp
from jax import lax
from jax.experimental import pallas as pl
from jax.experimental.pallas import tpu as pltpu
from jax.sharding import PartitionSpec as P

LAYER = 64
DOF = 64
ROWS = LAYER * DOF
K = 128
CORES = 2
XS = 4
ZS = 8
YS = 4
SPACE = ZS * XS * CORES
NARROW = K // YS
SIDES = 7
PARTS = 4
PART = ROWS // PARTS
HALF = ROWS // 2
NONE = 3 * LAYER
STEPS = (4, 3, 5, 2, 6, 1, 7)
WIDE = 32
SUB = 16
CHUNK = 1024
STAGED = 16
MESH = pl.DeviceIdType.MESH
F32 = jnp.float32
BF16 = jnp.bfloat16


def dot(left, right, left_dim, right_dim):
    return lax.dot_general(
        left,
        right,
        (((left_dim,), (right_dim,)), ((), ())),
        precision=lax.Precision.HIGHEST,
        preferred_element_type=F32,
    )


def times(left, right):
    return dot(left, right, 1, 0)


def cross(left, right):
    return dot(left, right, 1, 1)


def split(value):
    first = value.astype(BF16)
    rest = value - first.astype(F32)
    second = rest.astype(BF16)
    return first, second, (rest - second.astype(F32)).astype(BF16)


def eliminate(gram, unit, first):
    shape = gram.shape
    row_id = lax.broadcasted_iota(jnp.int32, shape, 0)
    for sub in range(0, WIDE, SUB):
        columns = [
            jnp.broadcast_to(gram[:, first + sub + j : first + sub + j + 1], shape)
            for j in range(SUB)
        ]
        for j in range(SUB):
            k = sub + j
            scale = lax.rsqrt(jnp.broadcast_to(columns[j][k : k + 1], shape))
            pivot_gram = jnp.broadcast_to(gram[k : k + 1], shape) * scale
            pivot_unit = jnp.broadcast_to(unit[k : k + 1], shape) * scale
            below = jnp.where(row_id > k, columns[j], 0.0) * scale
            for other in range(j + 1, SUB):
                near = jnp.broadcast_to(columns[j][sub + other : sub + other + 1], shape)
                columns[other] = columns[other] - below * (near * scale)
            gram = jnp.where(row_id == k, pivot_gram, gram - below * pivot_gram)
            unit = jnp.where(row_id == k, pivot_unit, unit - below * pivot_unit)
    return gram, unit


def factor_rows(gram_ref, upper, inverse, first):
    row_id = lax.broadcasted_iota(jnp.int32, (WIDE, K), 0)
    col_id = lax.broadcasted_iota(jnp.int32, (WIDE, K), 1)
    rows = pl.ds(first, WIDE)
    gram = gram_ref[rows, :]
    unit = jnp.where(row_id + first == col_id, 1.0, 0.0)
    if first:
        above_gram = upper[pl.ds(0, first), :]
        above_unit = inverse[pl.ds(0, first), :]
        left = above_gram[:, first : first + WIDE]
        gram = gram - dot(left, above_gram, 0, 0)
        unit = unit - dot(left, above_unit, 0, 0)
    gram, unit = eliminate(gram, unit, first)
    upper[rows, :] = jnp.where(row_id + first <= col_id, gram, 0.0)
    inverse[rows, :] = unit


def factor_gram(gram_ref, upper, inverse):
    for first in range(0, K, WIDE):
        factor_rows(gram_ref, upper, inverse, first)


def prepare(staged, packed, base):
    def body(elem, carry):
        for pair in range(4):
            if pair < 3:
                right = staged[elem, 2 * pair + 1]
            else:
                right = jnp.zeros((DOF, DOF), F32)
            both = jnp.concatenate([staged[elem, 2 * pair], right], axis=1)
            for piece, value in enumerate(split(both)):
                packed[base + elem, piece, :, pair * 128 : (pair + 1) * 128] = value
        return carry

    lax.fori_loop(0, STAGED, body, 0, unroll=2)


def spread(source, elems, base, part):
    is_low = lax.broadcasted_iota(jnp.int32, (NARROW, 2 * DOF), 1) < DOF
    count = LAYER // 2 // PARTS

    def body(step, carry):
        pair = part * count + step
        straight = source[:, pl.ds(pl.multiple_of(pair * 128, 128), 128)]
        turned = pltpu.roll(straight, DOF, 1)
        for side, low, high in ((0, straight, turned), (1, turned, straight)):
            place = base + 2 * pair + side
            for piece, value in enumerate(split(jnp.where(is_low, low, 0.0))):
                elems[0, place, piece] = value
            for piece, value in enumerate(split(jnp.where(is_low, 0.0, high))):
                elems[1, place, piece] = value
        return carry

    lax.fori_loop(0, count, body, 0, unroll=8)


def solid(cavity, elem):
    return (1 - cavity[elem]).astype(F32)


def operate(faces, shift, cavity, elems, packed, out, own_rows, begin, end):
    def product(left, right):
        return lax.dot_general(
            left, right, (((1,), (1,)), ((), ())), preferred_element_type=F32
        )

    def one(elem):
        at = [LAYER + elem]
        for side in range(SIDES - 1):
            beside = faces[side, elem]
            at.append(jnp.where(beside < 0, NONE, jnp.clip(beside + shift, 0, NONE - 1)))
        pieces = []
        for piece in range(3):
            pairs = [
                elems[0, at[2 * pair], piece] + elems[1, at[2 * pair + 1], piece]
                for pair in range(3)
            ]
            pairs.append(elems[0, at[6], piece])
            pieces.append(jnp.concatenate(pairs, axis=1))
        three = product(jnp.concatenate(pieces, axis=0), packed[elem, 0])
        two = product(jnp.concatenate(pieces[:2], axis=0), packed[elem, 1])
        last = product(pieces[0], packed[elem, 2])
        small = three[2 * NARROW :] + two[NARROW:] + last
        value = three[:NARROW] + (three[NARROW : 2 * NARROW] + two[:NARROW] + small)
        return value * solid(cavity, elem)

    def body(pair, carry):
        cols = pl.ds(pl.multiple_of(pair * 128, 128), 128)
        out[own_rows, cols] = jnp.concatenate([one(2 * pair), one(2 * pair + 1)], axis=1)
        return carry

    lax.fori_loop(begin, end, body, 0, unroll=4)


def kernel(
    faces,
    cavity,
    start,
    blocks,
    residue_out,
    gram_out,
    coef_out,
    basis,
    image,
    second,
    send_0,
    low_0,
    high_0,
    send_1,
    low_1,
    high_1,
    elems,
    packed,
    staged,
    near_0,
    far_0,
    done_0,
    near_1,
    far_1,
    done_1,
    near_2,
    far_2,
    done_2,
    near_3,
    far_3,
    done_3,
    part_0,
    part_1,
    part_2,
    part_3,
    gram,
    upper,
    inverse,
    alpha,
    flip,
    update,
    residue_sem,
    start_sem,
    stage_sem,
    halo_send,
    halo_recv,
    rows_send,
    rows_recv,
    sums_send,
    sums_recv,
):
    space = lax.axis_index("space")
    blk = lax.axis_index("blk")
    core = lax.rem(space, CORES)
    spot = lax.rem(space, XS * CORES)
    plane = space // (XS * CORES)
    plane_base = plane * (XS * CORES)
    quad = blk * CORES + core
    right = lax.rem(blk + 1, YS)
    left = lax.rem(blk + YS - 1, YS)
    shift = LAYER - space * LAYER
    own_rows = pl.ds(pl.multiple_of(blk * NARROW, NARROW), NARROW)
    right_rows = pl.ds(pl.multiple_of(right * NARROW, NARROW), NARROW)
    left_rows = pl.ds(pl.multiple_of(left * NARROW, NARROW), NARROW)
    above = (lax.rem(space + 1, SPACE), blk)
    below = (lax.rem(space + SPACE - 1, SPACE), blk)
    near_ids = [lax.rem(spot + step, 8) for step in STEPS]
    near_devices = [(plane_base + near, blk) for near in near_ids]
    far_devices = [(lax.rem(plane + step, 8) * 8 + spot, blk) for step in STEPS]
    quads = [lax.rem(quad + step, 8) for step in STEPS]
    done_devices = [(space - core + lax.rem(q, CORES), q // CORES) for q in quads]

    def stage_copy(part):
        return pltpu.make_async_copy(
            blocks.at[pl.ds(part * STAGED, STAGED)], staged.at[part % 2], stage_sem.at[part % 2]
        )

    load_start = pltpu.make_async_copy(start, basis.at[own_rows], start_sem)
    load_start.start()
    stage_copy(0).start()
    stage_copy(1).start()
    barrier = pltpu.get_barrier_semaphore()
    for device in near_devices + far_devices + done_devices + [above, below]:
        pl.semaphore_signal(barrier, inc=1, device_id=device, device_id_type=MESH)

    def masked(array, rows, send, part):
        is_low = lax.broadcasted_iota(jnp.int32, (NARROW, 2 * DOF), 1) < DOF
        count = LAYER // 2 // PARTS
        for step in range(count):
            pair = part * count + step
            cols = pl.ds(pl.multiple_of(pair * 128, 128), 128)
            weight = jnp.where(is_low, solid(cavity, 2 * pair), solid(cavity, 2 * pair + 1))
            send[:, cols] = array[rows, cols] * weight

    def halo_copies(call, part, send, low, high):
        cols = pl.ds(pl.multiple_of(part * PART, PART), PART)
        return [
            pltpu.make_async_remote_copy(
                src_ref=send.at[:, cols],
                dst_ref=target.at[:, cols],
                send_sem=halo_send.at[call, way, part],
                recv_sem=halo_recv.at[call, way, part],
                device_id=device,
                device_id_type=MESH,
            )
            for way, target, device in ((0, low, above), (1, high, below))
        ]

    def rows_copy(call, slot, array, rows, half, target, source=None):
        place = array.at[rows, pl.ds(half * HALF, HALF)]
        return pltpu.make_async_remote_copy(
            src_ref=place if source is None else source.at[:, pl.ds(half * HALF, HALF)],
            dst_ref=place,
            send_sem=rows_send.at[call, slot],
            recv_sem=rows_recv.at[call, slot],
            device_id=(space, target),
            device_id_type=MESH,
        )

    def gather(call, array, half, source=None):
        copies = [
            rows_copy(call, 2 * half, array, own_rows, half, (right, left)[half], source),
            rows_copy(call, 2 * half + 1, array, own_rows, half, (left, right)[half], source),
        ]
        for copy in copies:
            copy.start()
        return copies

    def relay(call, array, copies):
        copies[0].wait_recv()
        onward = rows_copy(call, 4, array, left_rows, 0, right)
        onward.start()
        copies[2].wait_recv()
        back = rows_copy(call, 5, array, right_rows, 1, left)
        back.start()
        return copies + [onward, back]

    def gathered(copies):
        for slot, copy in enumerate(copies):
            if slot not in (0, 2):
                copy.wait_recv()
        for copy in copies:
            copy.wait_send()

    sent = []

    def wait(copies):
        for copy in copies:
            copy.wait_recv()
        sent.extend(copies)

    def exchange(call, stage, sources, slots, mine, devices):
        copies = []
        for step in range(7):
            copy = pltpu.make_async_remote_copy(
                src_ref=sources[step],
                dst_ref=slots.at[mine],
                send_sem=sums_send.at[call, stage, step],
                recv_sem=sums_recv.at[call, stage, step],
                device_id=devices[step],
                device_id_type=MESH,
            )
            copy.start()
            copies.append(copy)
        return copies

    def total(slots):
        value = slots[0]
        for slot in range(1, 8):
            value = value + slots[slot]
        return value

    def reduce_near(call, part, near):
        half = part.shape[0] // CORES
        sources = [
            part.at[pl.ds(pl.multiple_of(lax.rem(spot_id, CORES) * half, 8), half)]
            for spot_id in near_ids
        ]
        copies = exchange(call, 0, sources, near, spot, near_devices)
        near[spot] = part[pl.ds(pl.multiple_of(core * half, 8), half), :]
        return copies

    def reduce_far(call, copies, near, far):
        wait(copies)
        far[plane] = total(near)
        return exchange(call, 1, [far.at[plane]] * 7, far, plane, far_devices)

    def reduce_done(call, copies, far, done):
        wait(copies)
        done[quad] = total(far)
        return exchange(call, 2, [done.at[quad]] * 7, done, quad, done_devices)

    def square(done, which):
        rows = []
        for member in range(YS):
            panel = jnp.concatenate([done[2 * member], done[2 * member + 1]], axis=0)
            rows.append(panel[which * NARROW : (which + 1) * NARROW])
        return jnp.concatenate(rows, axis=0)

    def over_chunks(body, init):
        def step(chunk, carry):
            return body(pl.ds(pl.multiple_of(chunk * CHUNK, CHUNK), CHUNK), carry)

        return lax.fori_loop(0, ROWS // CHUNK, step, init)

    def over_parts(body):
        def step(part, carry):
            body(part)
            return carry

        lax.fori_loop(0, PARTS, step, 0)

    def keep_upper(which):
        flip[...] = upper[...].T
        coef_out[which] = flip[own_rows, :]

    def receive(call, send, low, high, first, count):
        def body(step, carry):
            part = first + step
            for copy in halo_copies(call, part, send, low, high):
                copy.wait()
            spread(low, elems, 0, part)
            spread(high, elems, 2 * LAYER, part)
            return carry

        lax.fori_loop(0, count, body, 0)

    def apply(out, begin, end):
        operate(faces, shift, cavity, elems, packed, out, own_rows, begin, end)

    load_start.wait()
    over_parts(lambda part: masked(basis, own_rows, send_0, part))
    pl.semaphore_wait(barrier, 23)
    start_copies = gather(0, basis, 0, start) + gather(0, basis, 1, start)

    def start_halo(part):
        for copy in halo_copies(0, part, send_0, low_0, high_0):
            copy.start()

    over_parts(start_halo)
    for part in range(LAYER // STAGED):
        stage_copy(part).wait()
        prepare(staged.at[part % 2], packed, part * STAGED)
        if part + 2 < LAYER // STAGED:
            stage_copy(part + 2).start()
    for which in range(2):
        for piece in range(3):
            elems[which, NONE, piece] = jnp.zeros((NARROW, 2 * DOF), BF16)
    over_parts(lambda part: spread(send_0, elems, LAYER, part))
    start_copies = relay(0, basis, start_copies)
    receive(0, send_0, low_0, high_0, 0, PARTS)
    apply(image, 0, LAYER // 2)
    gathered(start_copies)
    image_copies = gather(1, image, 0) + gather(1, image, 1)

    def start_products(cols, carry):
        own = jnp.concatenate([basis[own_rows, cols], image[own_rows, cols]], axis=0)
        return carry + cross(own, basis[:, cols])

    part_0[...] = over_chunks(start_products, jnp.zeros(part_0.shape, F32))
    sums = reduce_near(0, part_0, near_0)
    sums = reduce_far(0, sums, near_0, far_0)
    sums = reduce_done(0, sums, far_0, done_0)
    image_copies = relay(1, image, image_copies)
    wait(sums)
    gram[...] = square(done_0, 0)
    factor_gram(gram, upper, inverse)
    alpha[...] = cross(times(inverse[...], square(done_0, 1)), inverse[...])
    update[:, pl.ds(0, K)] = inverse[...]
    update[:, pl.ds(K, K)] = -times(alpha[...], inverse[...])
    gathered(image_copies)

    def first_residue(part):
        for side in range(PART // CHUNK):
            cols = pl.ds(pl.multiple_of(part * PART + side * CHUNK, CHUNK), CHUNK)
            both = jnp.concatenate([image[:, cols], basis[:, cols]], axis=0)
            image[:, cols] = times(update[...], both)
        masked(image, own_rows, send_1, part)
        for copy in halo_copies(1, part, send_1, low_1, high_1):
            copy.start()

    over_parts(first_residue)

    def residue_products(cols, carry):
        own = image[own_rows, cols]
        vectors = times(inverse[...], basis[:, cols])
        basis[:, cols] = vectors
        return carry[0] + cross(own, image[:, cols]), carry[1] + cross(own, vectors)

    empty = jnp.zeros((NARROW, K), F32)
    products = over_chunks(residue_products, (empty, empty))
    part_1[pl.ds(0, NARROW), :] = products[0]
    part_1[pl.ds(NARROW, NARROW), :] = products[1]
    sums = reduce_near(1, part_1, near_1)
    over_parts(lambda part: spread(send_1, elems, LAYER, part))
    receive(1, send_1, low_1, high_1, 0, PARTS)
    sums = reduce_far(1, sums, near_1, far_1)
    apply(second, 0, LAYER // 4)
    second_copies = gather(2, second, 0)
    apply(second, LAYER // 4, LAYER // 2)
    sums = reduce_done(1, sums, far_1, done_1)
    second_copies += gather(2, second, 1)

    def image_products(cols, carry):
        return carry + cross(second[own_rows, cols], image[:, cols])

    part_2[...] = over_chunks(image_products, empty)
    inner_sums = reduce_near(2, part_2, near_2)
    coef_out[1] = alpha[own_rows, :]
    keep_upper(0)
    wait(sums)
    gram[...] = square(done_1, 0)
    inner_sums = reduce_far(2, inner_sums, near_2, far_2)
    second_copies = relay(2, second, second_copies)
    factor_gram(gram, upper, inverse)
    skew = cross(upper[...], times(inverse[...], square(done_1, 1)))
    inner_sums = reduce_done(2, inner_sums, far_2, done_2)
    update[:, pl.ds(0, K)] = inverse[...]

    def second_basis(cols, carry):
        image[:, cols] = times(inverse[...], image[:, cols])
        basis[:, cols] = times(upper[...], basis[:, cols])
        return carry

    over_chunks(second_basis, 0)
    keep_upper(2)
    wait(inner_sums)
    inner = cross(times(inverse[...], square(done_2, 0)), inverse[...])
    alpha[...] = inner - skew
    update[:, pl.ds(K, K)] = -alpha[...]
    gathered(second_copies)

    def second_residue(cols, carry):
        both = jnp.concatenate([second[:, cols], image[:, cols]], axis=0)
        value = times(update[...], both) - basis[:, cols]
        second[:, cols] = value
        return carry + cross(second[own_rows, cols], value)

    part_3[...] = over_chunks(second_residue, empty)
    sums = reduce_near(3, part_3, near_3)
    store_residue = pltpu.make_async_copy(second, residue_out, residue_sem)
    store_residue.start()
    coef_out[3] = alpha[own_rows, :]
    sums = reduce_far(3, sums, near_3, far_3)
    wait(reduce_done(3, sums, far_3, done_3))
    gram_out[...] = square(done_3, 0)
    store_residue.wait()
    for copy in sent:
        copy.wait_send()


def finish_kernel(residue, gram, coef, basis_out, coef_out, vectors, upper, inverse, flip, sem):
    own_rows = pl.ds(pl.multiple_of(lax.axis_index("blk") * NARROW, NARROW), NARROW)
    load = pltpu.make_async_copy(residue, vectors, sem)
    load.start()
    coef_out[pl.ds(0, 4)] = coef[...]
    factor_gram(gram, upper, inverse)
    flip[...] = upper[...].T
    coef_out[4] = flip[own_rows, :]
    load.wait()

    def last_basis(chunk, carry):
        cols = pl.ds(pl.multiple_of(chunk * CHUNK, CHUNK), CHUNK)
        basis_out[:, cols] = times(inverse[own_rows, :], vectors[:, cols])
        return carry

    lax.fori_loop(0, ROWS // CHUNK, last_basis, 0)


def local(start, faces, cavity, blocks):
    smem = pl.BlockSpec(memory_space=pltpu.SMEM)
    vmem = pl.BlockSpec(memory_space=pltpu.VMEM)

    def slots(rows):
        return [pltpu.VMEM((8, rows // CORES, K), F32)] * 3

    residue, gram, coefficients = pl.pallas_call(
        kernel,
        out_shape=(
            jax.ShapeDtypeStruct((K, ROWS), F32),
            jax.ShapeDtypeStruct((K, K), F32),
            jax.ShapeDtypeStruct((4, NARROW, K), F32),
        ),
        in_specs=[
            smem,
            smem,
            pl.BlockSpec(memory_space=pl.ANY),
            pl.BlockSpec(memory_space=pl.ANY),
        ],
        out_specs=(pl.BlockSpec(memory_space=pl.ANY), vmem, vmem),
        scratch_shapes=[pltpu.VMEM((K, ROWS), F32)] * 3
        + [pltpu.VMEM((NARROW, ROWS), F32)] * 6
        + [
            pltpu.VMEM((2, NONE + 1, 3, NARROW, 2 * DOF), BF16),
            pltpu.VMEM((LAYER, 3, DOF, 8 * DOF), BF16),
            pltpu.VMEM((2, STAGED, SIDES, DOF, DOF), F32),
        ]
        + slots(2 * NARROW)
        + slots(2 * NARROW)
        + slots(NARROW)
        + slots(NARROW)
        + [pltpu.VMEM((count * NARROW, K), F32) for count in (2, 2, 1, 1)]
        + [pltpu.VMEM((K, K), F32)] * 5
        + [pltpu.VMEM((K, 2 * K), F32)]
        + [
            pltpu.SemaphoreType.DMA,
            pltpu.SemaphoreType.DMA,
            pltpu.SemaphoreType.DMA((2,)),
            pltpu.SemaphoreType.DMA((2, 2, PARTS)),
            pltpu.SemaphoreType.DMA((2, 2, PARTS)),
            pltpu.SemaphoreType.DMA((3, 6)),
            pltpu.SemaphoreType.DMA((3, 6)),
            pltpu.SemaphoreType.DMA((4, 3, 7)),
            pltpu.SemaphoreType.DMA((4, 3, 7)),
        ],
        compiler_params=pltpu.CompilerParams(
            collective_id=1, has_side_effects=True, vmem_limit_bytes=60 * 2**20
        ),
    )(faces.T, cavity, start.T, blocks)
    basis, coefficients = pl.pallas_call(
        finish_kernel,
        out_shape=(
            jax.ShapeDtypeStruct((NARROW, ROWS), F32),
            jax.ShapeDtypeStruct((5, NARROW, K), F32),
        ),
        in_specs=[pl.BlockSpec(memory_space=pl.ANY), vmem, vmem],
        out_specs=(vmem, vmem),
        scratch_shapes=[pltpu.VMEM((K, ROWS), F32)]
        + [pltpu.VMEM((K, K), F32)] * 3
        + [pltpu.SemaphoreType.DMA],
        compiler_params=pltpu.CompilerParams(vmem_limit_bytes=63 * 2**20),
    )(residue, gram, coefficients)
    return basis.T, jnp.swapaxes(coefficients, 1, 2)


def solution(mesh):
    in_specs = (P("space", "blk"), P("space", None), P("space"), P("space", None, None, None))
    out_specs = (P("space", "blk"), P(None, None, "blk"))
    return jax.shard_map(local, mesh=mesh, in_specs=in_specs, out_specs=out_specs, check_vma=False)
```
